256 devices in a mesh: row: 16 (over y, x_lo, core), col: 16 (over z, x_hi).
Axes of the slice: x: 4 (x_hi: 2, x_lo: 2; x = x_hi * 2 + x_lo), y: 4, z: 8, core: 2. Of those that a mesh axis runs over, the one named last changes fastest.
Arguments:
- features: bfloat16 [1024, 128], P(('row', 'col')), may hold values from -6 to 6
- w_left: bfloat16 [128, 128], replicated, may hold values from -0.5 to 0.5
- w_right: bfloat16 [128, 128], replicated, may hold values from -0.5 to 0.5
- w_in: bfloat16 [32, 128], replicated, may hold values from -0.5 to 0.5
- pair_input: bfloat16 [32, 1024, 1024], P(None, 'row', 'col'), may hold values from -6 to 6
- conv_w: bfloat16 [3, 32, 288], replicated, may hold values from -0.375 to 0.375
- w_out: bfloat16 [32], replicated, may hold values from -1 to 1
- dilation: int32 [3], replicated, may hold values from 1 to 8, as said below
- cotangent: float32 [1024, 1024], P('row', 'col'), may hold values from -6 to 6
Outputs:
- logits: float32 [1024, 1024], P('row', 'col')
- grad_rows: float32 [1024, 128], P('row')
- grad_cols: float32 [1024, 128], P('col')
- conv_grads: float32 [3, 32, 288], replicated
The draws below stay inside these ranges and needn't reach their ends.
Inputs may be any that keep to these rules, and one draw needn't show every extreme that they name: `dilation`: every layer's rate lies in 1 .. 8; at least one layer has rate 8 and another layer has rate 1.
All inputs are finite; a program needn't handle non-finite values.
Results may differ from the reference program's by a relative error of at most 0.02.
Values may be sent and summed in bfloat16 or wider, within the bound.
No kernel may reach another device: no remote copies, remote signals or barrier semaphores. Data moves between devices by JAX's collectives and lax.ppermute only.
A program may use at most 128 MiB of HBM per device.

```python
import jax
import jax.numpy as jnp
from jax import lax

FEAT = 128
CH = 32
LAYERS = 3
RMAX = 8
TR = 64
L = 1024
N_ROW = 16


def draw_dilation(key, part):
    key = jax.random.fold_in(key, 7)
    first_key, second_key, third_key = jax.random.split(key, 3)
    rates = jax.random.randint(first_key, (LAYERS,), 1, RMAX + 1)
    chosen = jax.random.randint(second_key, (), 0, LAYERS)
    step_on = jax.random.randint(third_key, (), 1, LAYERS)
    other = (chosen + step_on) % LAYERS
    positions = jnp.arange(LAYERS)
    rates = jnp.where(positions == other, 1, rates)
    rates = jnp.where(positions == chosen, RMAX, rates)
    return rates.astype(jnp.int32)


def block_levels(own_key, extent, shards, low, largest):
    def one(position, blocks):
        heights = jax.random.uniform(jax.random.fold_in(jax.random.fold_in(own_key, 6), position), (blocks,), jnp.float32, low / len(shards), largest / len(shards))
        return jnp.repeat(jnp.exp(heights), extent[position] // blocks).reshape((-1,) + (1,) * (len(extent) - position - 1))

    loudness = one(*shards[0])
    for cut in shards[1:]:
        loudness = loudness * one(*cut)
    return loudness


def bell_draw(rng, extent, width, bound, cuts=(), kind=jnp.bfloat16):
    values = width * jax.random.normal(rng, extent, jnp.float32)
    if cuts:
        values = values * block_levels(rng, extent, cuts, -0.22, 0.18)
    return jnp.clip(values, -bound, bound).astype(kind)


def setup_inputs(seed: int = 0) -> dict:
    arg_keys = jax.random.split(jax.random.key(seed), 10)
    return {
        "features": bell_draw(arg_keys[0], (L, FEAT), 1.0, 6.0, ((0, 256),)),
        "w_left": bell_draw(arg_keys[1], (FEAT, FEAT), FEAT ** -0.5, 0.5),
        "w_right": bell_draw(arg_keys[2], (FEAT, FEAT), FEAT ** -0.5, 0.5),
        "w_in": bell_draw(arg_keys[3], (CH, FEAT), FEAT ** -0.5, 0.5),
        "pair_input": bell_draw(arg_keys[4], (CH, L, L), 1.0, 6.0, ((1, 16), (2, 16))),
        "conv_w": bell_draw(arg_keys[5], (LAYERS, CH, 9 * CH), (9 * CH) ** -0.5, 0.375),
        "w_out": bell_draw(arg_keys[6], (CH,), CH ** -0.5, 1.0),
        "dilation": draw_dilation(jax.random.fold_in(arg_keys[9], 71), 0),
        "cotangent": bell_draw(arg_keys[8], (L, L), 1.0, 6.0, ((0, 16), (1, 16)), jnp.float32),
    }


K_ROOT = 0.7978845608028654
CUBIC = 0.044715


def gelu_pair(value):
    inner = K_ROOT * (value + CUBIC * value * value * value)
    tangent = jnp.tanh(inner)
    result = 0.5 * value * (1.0 + tangent)
    slope = 0.5 * (1.0 + tangent) + 0.5 * value * (1.0 - tangent * tangent) * K_ROOT * (1.0 + 3.0 * CUBIC * value * value)
    return result, slope


def patches(padded, rate, sign, rows, cols):
    depth = padded.shape[0]
    pieces = []
    for down in (-1, 0, 1):
        for across in (-1, 0, 1):
            first = (RMAX + sign * down * rate).astype(jnp.int32)
            second = (RMAX + sign * across * rate).astype(jnp.int32)
            pieces.append(lax.dynamic_slice(padded, (jnp.int32(0), first, second), (depth, rows, cols)))
    return jnp.concatenate(pieces, 0).reshape(9 * depth, rows * cols)


def flipped(weight):
    channels = weight.shape[0]
    return weight.reshape(channels, 9, channels).transpose(2, 1, 0).reshape(channels, 9 * channels)


def regroup(blocks):
    return blocks.transpose(1, 0, 2, 3).reshape(blocks.shape[1], blocks.shape[0] * blocks.shape[2], blocks.shape[3])


def reference(features, w_left, w_right, w_in, pair_input, conv_w, w_out, dilation, cotangent):
    length = features.shape[0]
    row_project = jnp.dot(features, w_left, preferred_element_type=jnp.float32)
    col_project = jnp.dot(features, w_right, preferred_element_type=jnp.float32)
    starts = jnp.arange(N_ROW, dtype=jnp.int32) * TR

    def first_block(start):
        rows_proj = lax.dynamic_slice_in_dim(row_project, start, TR, 0)
        outer = rows_proj.T[:, :, None] + col_project.T[:, None, :]
        hidden = gelu_pair(outer)[0].astype(jnp.bfloat16)
        mixed = jnp.dot(w_in, hidden.reshape(FEAT, TR * length), preferred_element_type=jnp.float32)
        given = lax.dynamic_slice_in_dim(pair_input, start, TR, 1).astype(jnp.float32)
        return (mixed.reshape(CH, TR, length) + given).astype(jnp.bfloat16)

    state = regroup(lax.map(first_block, starts))
    saved_state = []
    saved_pad = []
    for layer in range(LAYERS):
        activated = gelu_pair(state.astype(jnp.float32))[0].astype(jnp.bfloat16)
        padded = jnp.pad(activated, ((0, 0), (RMAX, RMAX), (RMAX, RMAX)))
        rate = dilation[layer]
        weight = conv_w[layer]

        def conv_block(start, padded=padded, rate=rate, weight=weight):
            window = lax.dynamic_slice(padded, (jnp.int32(0), start, jnp.int32(0)), (CH, TR + 2 * RMAX, length + 2 * RMAX))
            out = jnp.dot(weight, patches(window, rate, 1, TR, length), preferred_element_type=jnp.float32)
            return out.reshape(CH, TR, length)

        update = regroup(lax.map(conv_block, starts))
        saved_state.append(state)
        saved_pad.append(padded)
        state = (state.astype(jnp.float32) + update).astype(jnp.bfloat16)
    direct = jnp.dot(w_out, state.reshape(CH, length * length), preferred_element_type=jnp.float32).reshape(length, length)
    logits = 0.5 * (direct + direct.T)
    upstream = 0.5 * (cotangent + cotangent.T)
    grad_state = upstream[None, :, :] * w_out.astype(jnp.float32)[:, None, None]
    weight_grads = []
    for layer in reversed(range(LAYERS)):
        rounded = grad_state.astype(jnp.bfloat16)
        grad_pad = jnp.pad(rounded, ((0, 0), (RMAX, RMAX), (RMAX, RMAX)))
        rate = dilation[layer]
        back_weight = flipped(conv_w[layer])
        padded = saved_pad[layer]

        def grad_block(start, padded=padded, grad_pad=grad_pad, rounded=rounded, rate=rate, back_weight=back_weight):
            window = lax.dynamic_slice(padded, (jnp.int32(0), start, jnp.int32(0)), (CH, TR + 2 * RMAX, length + 2 * RMAX))
            grad_window = lax.dynamic_slice(grad_pad, (jnp.int32(0), start, jnp.int32(0)), (CH, TR + 2 * RMAX, length + 2 * RMAX))
            rows_grad = lax.dynamic_slice_in_dim(rounded, start, TR, 1).reshape(CH, TR * length)
            term = lax.dot_general(rows_grad, patches(window, rate, 1, TR, length), (((1,), (1,)), ((), ())), preferred_element_type=jnp.float32)
            back = jnp.dot(back_weight, patches(grad_window, rate, -1, TR, length), preferred_element_type=jnp.float32)
            return term, back.reshape(CH, TR, length)

        terms, backs = lax.map(grad_block, starts)
        weight_grads.insert(0, jnp.sum(terms, 0) / length)
        slope = gelu_pair(saved_state[layer].astype(jnp.float32))[1]
        grad_state = grad_state + regroup(backs) * slope
    rounded_start = grad_state.astype(jnp.bfloat16)

    def feature_block(start):
        rows_proj = lax.dynamic_slice_in_dim(row_project, start, TR, 0)
        outer = rows_proj.T[:, :, None] + col_project.T[:, None, :]
        slope = gelu_pair(outer)[1]
        rows_grad = lax.dynamic_slice_in_dim(rounded_start, start, TR, 1).reshape(CH, TR * length)
        hidden_grad = lax.dot_general(w_in, rows_grad, (((0,), (0,)), ((), ())), preferred_element_type=jnp.float32)
        outer_grad = hidden_grad.reshape(FEAT, TR, length) * slope
        return jnp.sum(outer_grad, 2).T, jnp.sum(outer_grad, 1).T

    row_parts, col_parts = lax.map(feature_block, starts)
    row_sum = row_parts.reshape(length, FEAT)
    col_sum = jnp.sum(col_parts, 0)
    grad_rows = jnp.dot(row_sum, w_left.astype(jnp.float32).T, precision=lax.Precision.HIGHEST)
    grad_cols = jnp.dot(col_sum, w_right.astype(jnp.float32).T, precision=lax.Precision.HIGHEST)
    conv_grads = jnp.stack(weight_grads)
    return logits, grad_rows, grad_cols, conv_grads
```

```python
import jax
import jax.numpy as jnp
from jax import lax
from jax.experimental import pallas as pl
from jax.experimental.pallas import tpu as pltpu
from jax.sharding import PartitionSpec as P

F32 = jnp.float32
BF16 = jnp.bfloat16
K_ROOT = 0.7978845608028654
CUBIC = 0.044715
TILE = 64
HALO = 32
WIDE = TILE + 2 * HALO
CH = 32
VMEM = pl.BlockSpec(memory_space=pltpu.VMEM)
SMEM = pl.BlockSpec(memory_space=pltpu.SMEM)


def gelu(value):
    inner = value * (K_ROOT + (K_ROOT * CUBIC) * (value * value))
    half = 0.5 * value
    return half + half * jnp.tanh(inner)


def gelu_pair(value):
    square = value * value
    tangent = jnp.tanh(value * (K_ROOT + (K_ROOT * CUBIC) * square))
    half = 0.5 * value
    up = 0.5 + 0.5 * tangent
    result = value * up
    slope = up + half * (1.0 - tangent * tangent) * (K_ROOT + (3.0 * K_ROOT * CUBIC) * square)
    return result, slope


def split(value):
    high = value.astype(BF16)
    return high, (value - high.astype(F32)).astype(BF16)


def edges_kernel(pair_ref, cot_ref, own_ref, left_ref, right_ref):
    own = jnp.swapaxes(pair_ref[...].astype(F32), 0, 1)
    own_ref[...] = own.astype(BF16)
    cot = cot_ref[...]
    for out_ref, first in ((left_ref, 0), (right_ref, TILE - HALO)):
        last = first + HALO
        for q in range(16):
            out_ref[q] = jnp.concatenate(
                [own[q + 16 * m, :, first:last] for m in range(4)], axis=1
            ).astype(BF16)
        edge = jnp.concatenate([cot[16 * m : 16 * m + 16, first:last] for m in range(4)], axis=1)
        high, low = split(edge)
        out_ref[16, 0:16, :] = high
        out_ref[16, 16:32, :] = low


def widen_kernel(own_ref, cot_ref, from_left_ref, from_right_ref, upper_ref, lower_ref):
    cot = cot_ref[...]
    for m in range(4):
        out_ref = (upper_ref, lower_ref)[m // 2]
        lanes = slice(HALO * m, HALO * m + HALO)
        base = 16 * (m % 2)
        for q in range(16):
            out_ref[base + q] = jnp.concatenate(
                [
                    own_ref[16 * m + q].astype(F32),
                    from_right_ref[q].astype(F32)[:, lanes],
                    from_left_ref[q].astype(F32)[:, lanes],
                ],
                axis=1,
            ).astype(BF16)
        high, low = split(cot[16 * m : 16 * m + 16, :])
        for part, row, at in ((high, 32, 0), (low, 33, 16)):
            out_ref[row, base : base + 16, :] = jnp.concatenate(
                [
                    part.astype(F32),
                    from_right_ref[16, at : at + 16, :].astype(F32)[:, lanes],
                    from_left_ref[16, at : at + 16, :].astype(F32)[:, lanes],
                ],
                axis=1,
            ).astype(BF16)


def mixed_kernel(place_ref, feat_ref, w_left_ref, w_right_ref, w_in_ref, mixed_ref, rows_ref, cols_ref):
    row = place_ref[0]
    col = place_ref[1]
    row_chunks = [jnp.maximum(2 * row - 1, 0), 2 * row, 2 * row + 1, jnp.minimum(2 * row + 2, 31)]
    col_chunks = [2 * col, 2 * col + 1, jnp.minimum(2 * col + 2, 31), jnp.maximum(2 * col - 1, 0)]
    for chunks, weight_ref, out_ref in (
        (row_chunks, w_left_ref, rows_ref),
        (col_chunks, w_right_ref, cols_ref),
    ):
        picked = jnp.concatenate([feat_ref[chunk] for chunk in chunks], axis=0)
        out_ref[...] = jnp.dot(picked, weight_ref[...], preferred_element_type=F32)
    w_in = w_in_ref[...]

    def body(step, carry):
        for k in range(2):
            pair = []
            for i in range(2):
                outer = rows_ref[pl.ds(4 * step + 2 * k + i, 1), :] + cols_ref[...]
                pair.append(gelu(outer).astype(BF16))
            out = lax.dot_general(
                w_in, jnp.concatenate(pair, 0), (((1,), (1,)), ((), ())), preferred_element_type=F32
            )
            for i in range(2):
                mixed_ref[4 * step + 2 * k + i] = out[:, WIDE * i : WIDE * i + WIDE]
        return carry

    lax.fori_loop(0, WIDE // 4, body, 0)


def shifted(value, rate):
    return jnp.concatenate(
        [pltpu.roll(value, rate, 1), value, pltpu.roll(value, WIDE - rate, 1)], axis=0
    ).astype(BF16)


def lane_mask(col):
    lane = lax.broadcasted_iota(jnp.int32, (1, WIDE), 1)
    bin_at = TILE * col + jnp.where(lane < TILE + HALO, lane, lane - WIDE)
    return jnp.where((bin_at >= 0) & (bin_at < 1024), 1.0, 0.0).astype(F32)


def row_valid(row, i):
    at = TILE * row - HALO + i
    return jnp.where((at >= 0) & (at < 1024), 1.0, 0.0).astype(F32)


def gather_taps(z_ref, i, rate):
    return z_ref[i - rate, 0:CH, :] + z_ref[i, CH : 2 * CH, :] + z_ref[i + rate, 2 * CH : 3 * CH, :]


def rows_loop(first, last, one, many):
    def body(step, carry):
        base = first + 4 * step
        for k in range(2):
            i = base + 2 * k
            many(i, jnp.concatenate([one(i), one(i + 1)], axis=1))
        return carry

    lax.fori_loop(0, (last - first) // 4, body, 0)


def main_kernel(
    place_ref,
    mixed_ref,
    part0_ref,
    part1_ref,
    part2_ref,
    part3_ref,
    mirror_ref,
    forward_ref,
    backward_ref,
    w_out_ref,
    direct_ref,
    terms_ref,
    grad_ref,
    round_ref,
    slope0_ref,
    state_ref,
    slope1_ref,
    slope2_ref,
    za_ref,
    zb_ref,
    patch0_ref,
    patch1_ref,
    patch2_ref,
    masked_ref,
    upstream_ref,
    grad2_ref,
):
    row = place_ref[0]
    col = place_ref[1]
    rates = [place_ref[2], place_ref[3], place_ref[4]]
    inside = lane_mask(col)
    patch_refs = (patch0_ref, patch1_ref, patch2_ref)
    parts = (part0_ref, part1_ref, part2_ref, part3_ref)
    w_out = w_out_ref[...]
    z_refs = (za_ref, zb_ref)

    for n in range(4):

        def start(q, carry, n=n):
            given = parts[n][q].astype(F32)
            state_ref[HALO * n + q] = (mixed_ref[HALO * n + q] + given).astype(BF16)
            return carry

        lax.fori_loop(0, HALO, start, 0, unroll=4)

    def activate(layer, i, state):
        act, slope = gelu_pair(state)
        if layer == 0:
            slope0_ref[i] = slope
        else:
            (slope1_ref, slope2_ref)[layer - 1][i] = slope
        return shifted(act * (inside * row_valid(row, i)), rates[layer])

    for layer in range(3):
        z_now = z_refs[layer % 2]
        z_last = z_refs[(layer + 1) % 2]

        def one(i, layer=layer, z_last=z_last):
            if layer == 0:
                state = state_ref[i].astype(F32)
            else:
                new = state_ref[i].astype(F32) + gather_taps(z_last, i, rates[layer - 1])
                new = new.astype(BF16)
                state_ref[i] = new
                state = new.astype(F32)
            out = activate(layer, i, state)
            patch_refs[layer][i] = out
            return out

        def many(i, pair, layer=layer, z_now=z_now):
            z = jnp.dot(forward_ref[layer], pair, preferred_element_type=F32)
            z_now[i] = z[:, :WIDE]
            z_now[i + 1] = z[:, WIDE:]

        rows_loop(8 * layer, WIDE - 8 * layer, one, many)

    def finish(i, carry):
        new = state_ref[i].astype(F32) + gather_taps(za_ref, i, rates[2])
        new = new.astype(BF16).astype(F32)
        direct_ref[pl.ds(i - HALO, 1), :] = jnp.sum(new * w_out, axis=0, keepdims=True)[:, :TILE]
        return carry

    lax.fori_loop(HALO, HALO + TILE, finish, 0, unroll=4)

    other = mirror_ref[...].T
    other = jnp.concatenate([other[96:128], other[0:96]], axis=0)
    other = jnp.concatenate([other[:, 32:128], other[:, 0:32]], axis=1)
    for n in range(4):
        mine = parts[n][32].astype(F32) + parts[n][33].astype(F32)
        rows = slice(HALO * n, HALO * n + HALO)
        upstream_ref[rows, :] = 0.5 * (mine + other[rows, :])

    tile_lanes = jnp.where(lax.broadcasted_iota(jnp.int32, (1, WIDE), 1) < TILE, 1.0, 0.0).astype(F32)
    terms_ref[...] = jnp.zeros_like(terms_ref)
    masked_ref[...] = jnp.zeros_like(masked_ref)

    def weight_terms(layer):
        def keep(i, carry):
            masked_ref[i] = (round_ref[i].astype(F32) * tile_lanes).astype(BF16)
            return carry

        lax.fori_loop(HALO, HALO + TILE, keep, 0, unroll=4)
        rate = rates[layer]

        def body(step, total):
            base = 24 + 4 * step
            left = jnp.concatenate(
                [
                    jnp.concatenate([masked_ref[base + k + off] for k in range(4)], axis=1)
                    for off in (rate, 0, -rate)
                ],
                axis=0,
            )
            right = jnp.concatenate([patch_refs[layer][base + k] for k in range(4)], axis=1)
            return total + lax.dot_general(
                left, right, (((1,), (1,)), ((), ())), preferred_element_type=F32
            )

        terms_ref[layer] = lax.fori_loop(0, 20, body, jnp.zeros((96, 96), F32))

    def back(layer, first, last, one_grad, z_now):
        def one(i):
            rounded = one_grad(i).astype(BF16)
            round_ref[i] = rounded
            return shifted(rounded.astype(F32), rates[layer])

        def many(i, pair):
            z = jnp.dot(backward_ref[layer], pair, preferred_element_type=F32)
            z_now[i] = z[:, :WIDE]
            z_now[i + 1] = z[:, WIDE:]

        rows_loop(first, last, one, many)
        weight_terms(layer)

    def first_grad(i):
        return upstream_ref[pl.ds(i, 1), :] * w_out

    def second_grad(i):
        new = first_grad(i) + gather_taps(zb_ref, i, rates[2]) * slope2_ref[i]
        new = new * (inside * row_valid(row, i))
        grad2_ref[i] = new
        return new

    back(2, 8, 120, first_grad, zb_ref)
    back(1, 16, 112, second_grad, za_ref)

    def third_grad(i, carry):
        new = grad2_ref[i] + gather_taps(za_ref, i, rates[1]) * slope1_ref[i]
        new = new * (inside * row_valid(row, i))
        grad_ref[i] = new
        round_ref[i] = new.astype(BF16)
        return carry

    lax.fori_loop(24, 104, third_grad, 0, unroll=4)
    weight_terms(0)


def last_kernel(
    place_ref,
    grad_ref,
    round_ref,
    slope0_ref,
    rows_ref,
    cols_ref,
    backward_ref,
    w_in_ref,
    row_ref,
    col_ref,
    z_ref,
):
    rate = place_ref[2]

    def one(i):
        return shifted(round_ref[i].astype(F32), rate)

    def many(i, pair):
        z = jnp.dot(backward_ref[0], pair, preferred_element_type=F32)
        z_ref[i] = z[:, :WIDE]
        z_ref[i + 1] = z[:, WIDE:]

    rows_loop(24, 104, one, many)
    w_in = w_in_ref[...]
    cols = cols_ref[0:TILE, :]

    def body(step, total):
        for k in range(2):
            i = HALO + 2 * step + k
            start = grad_ref[i] + gather_taps(z_ref, i, rate) * slope0_ref[i]
            hidden = lax.dot_general(
                start[:, :TILE].astype(BF16), w_in, (((0,), (0,)), ((), ())), preferred_element_type=F32
            )
            slope = gelu_pair(rows_ref[pl.ds(i, 1), :] + cols)[1]
            outer = hidden * slope
            row_ref[pl.ds(i - HALO, 1), :] = jnp.sum(outer, axis=0, keepdims=True)
            total = total + outer
        return total

    col_ref[...] = lax.fori_loop(0, TILE // 2, body, jnp.zeros((TILE, 128), F32))


def shape(*dims, dtype=F32):
    return jax.ShapeDtypeStruct(dims, dtype)


def call(kernel, outs, specs, scratch=()):
    return pl.pallas_call(
        kernel,
        out_shape=outs,
        in_specs=specs,
        out_specs=[VMEM] * len(outs),
        scratch_shapes=list(scratch),
        compiler_params=pltpu.CompilerParams(vmem_limit_bytes=56 * 2**20),
    )


def flips(axis, bit):
    return [(i, i ^ bit) for i in range(lax.axis_size(axis))]


def on_device(features, w_left, w_right, w_in, pair_input, conv_w, w_out, dilation, cotangent):
    n_row = lax.axis_size("row")
    n_col = lax.axis_size("col")
    row_at = lax.axis_index("row").astype(jnp.int32)
    col_at = lax.axis_index("col").astype(jnp.int32)
    place = jnp.concatenate([jnp.stack([row_at, col_at]), dilation, jnp.zeros((3,), jnp.int32)])
    up = [(i, i + 1) for i in range(n_row - 1)]
    down = [(i + 1, i) for i in range(n_row - 1)]
    swap = [(r * n_col + c, c * n_col + r) for r in range(n_row) for c in range(n_col)]

    own, left_edge, right_edge = call(
        edges_kernel,
        [shape(TILE, CH, TILE, dtype=BF16)] + [shape(17, CH, WIDE, dtype=BF16)] * 2,
        [VMEM] * 2,
    )(pair_input, cotangent)
    from_left = lax.ppermute(right_edge, "col", up)
    from_right = lax.ppermute(left_edge, "col", down)

    sent = jnp.broadcast_to(features.reshape(1, 1, 512), (n_row * n_col, 1, 512))
    gathered = lax.all_to_all(sent, ("row", "col"), 0, 0).reshape(32, 32, 128)

    upper, lower = call(
        widen_kernel, [shape(HALO + 2, CH, WIDE, dtype=BF16)] * 2, [VMEM] * 4
    )(own, cotangent, from_left, from_right)
    above = lax.ppermute(lower, "row", up)
    below = lax.ppermute(upper, "row", down)

    mixed, row_project, col_project = call(
        mixed_kernel,
        [shape(WIDE, CH, WIDE), shape(WIDE, 128), shape(WIDE, 128)],
        [SMEM] + [VMEM] * 4,
    )(place, gathered, w_left, w_right, w_in)

    wide_cot = jnp.concatenate(
        [part[32].astype(F32) + part[33].astype(F32) for part in (above, upper, lower, below)], axis=0
    )
    mirrored = lax.ppermute(wide_cot, ("row", "col"), swap)

    forward_w = conv_w.reshape(3, CH, 3, 3 * CH).transpose(0, 2, 1, 3).reshape(3, 96, 96)
    backward_w = (
        conv_w.reshape(3, CH, 3, 3, CH)[:, :, ::-1, ::-1, :].transpose(0, 2, 4, 3, 1).reshape(3, 96, 96)
    )
    w_out_wide = jnp.broadcast_to(w_out.astype(F32)[:, None], (CH, WIDE))
    big = (WIDE, CH, WIDE)
    direct, terms, grad, rounded, slope0 = call(
        main_kernel,
        [shape(TILE, TILE), shape(3, 96, 96), shape(*big), shape(*big, dtype=BF16), shape(*big)],
        [SMEM] + [VMEM] * 9,
        [
            pltpu.VMEM(big, BF16),
            pltpu.VMEM(big, F32),
            pltpu.VMEM(big, F32),
            pltpu.VMEM((WIDE, 96, WIDE), F32),
            pltpu.VMEM((WIDE, 96, WIDE), F32),
            pltpu.VMEM((WIDE, 96, WIDE), BF16),
            pltpu.VMEM((WIDE, 96, WIDE), BF16),
            pltpu.VMEM((WIDE, 96, WIDE), BF16),
            pltpu.VMEM(big, BF16),
            pltpu.VMEM((WIDE, WIDE), F32),
            pltpu.VMEM(big, F32),
        ],
    )(place, mixed, above, upper, lower, below, mirrored, forward_w, backward_w, w_out_wide)

    row_part, col_part = call(
        last_kernel,
        [shape(TILE, 128), shape(TILE, 128)],
        [SMEM] + [VMEM] * 7,
        [pltpu.VMEM((WIDE, 96, WIDE), F32)],
    )(place, grad, rounded, slope0, row_project, col_project, backward_w, w_in)

    other = lax.ppermute(direct, ("row", "col"), swap)
    logits = 0.5 * (direct + other.T)

    def summed(value, axis, bit):
        value = value.astype(BF16)
        return value.astype(F32) + lax.ppermute(value, axis, flips(axis, bit)).astype(F32)

    packed = terms.reshape(216, 128)
    for bit in (1, 2, 4, 8):
        packed = summed(packed, "row", bit)
        row_part = summed(row_part, "col", bit)
        col_part = summed(col_part, "row", bit)
    for bit in (1, 2, 4, 8):
        packed = summed(packed, "col", bit)
    conv_grads = (
        packed.reshape(3, 3, CH, 96).transpose(0, 2, 1, 3).reshape(3, CH, 288) / (TILE * n_row)
    )
    grad_rows = jnp.dot(row_part, w_left.astype(F32).T, precision=lax.Precision.HIGHEST)
    grad_cols = jnp.dot(col_part, w_right.astype(F32).T, precision=lax.Precision.HIGHEST)
    return (logits, grad_rows, grad_cols, conv_grads)


def solution(mesh):
    return jax.shard_map(
        on_device,
        mesh=mesh,
        in_specs=(
            P(("row", "col"), None),
            P(),
            P(),
            P(),
            P(None, "row", "col"),
            P(),
            P(),
            P(),
            P("row", "col"),
        ),
        out_specs=(P("row", "col"), P("row", None), P("col", None), P()),
        check_vma=False,
    )
```

```python
import jax
import jax.numpy as jnp
from jax import lax
from jax.experimental import pallas as pl
from jax.experimental.pallas import tpu as pltpu
from jax.sharding import PartitionSpec as P

F32 = jnp.float32
BF16 = jnp.bfloat16
K_ROOT = 0.7978845608028654
CUBIC = 0.044715
TILE = 64
HALO = 32
WIDE = TILE + 2 * HALO
CH = 32
ROWS = 16
VMEM = pl.BlockSpec(memory_space=pltpu.VMEM)
SMEM = pl.BlockSpec(memory_space=pltpu.SMEM)


def gelu(value):
    inner = value * (K_ROOT + (K_ROOT * CUBIC) * (value * value))
    half = 0.5 * value
    return half + half * jnp.tanh(inner)


def gelu_pair(value):
    square = value * value
    tangent = jnp.tanh(value * (K_ROOT + (K_ROOT * CUBIC) * square))
    half = 0.5 * value
    up = 0.5 + 0.5 * tangent
    result = value * up
    slope = up + half * (1.0 - tangent * tangent) * (K_ROOT + (3.0 * K_ROOT * CUBIC) * square)
    return result, slope


def split(value):
    high = value.astype(BF16)
    return high, (value - high.astype(F32)).astype(BF16)


def edges_kernel(pair_ref, cot_ref, own_ref, left_ref, right_ref):
    own = jnp.swapaxes(pair_ref[...].astype(F32), 0, 1)
    own_ref[...] = own.astype(BF16)
    cot = cot_ref[...]
    for out_ref, first in ((left_ref, 0), (right_ref, TILE - HALO)):
        last = first + HALO
        for q in range(16):
            out_ref[q] = jnp.concatenate(
                [own[q + 16 * m, :, first:last] for m in range(4)], axis=1
            ).astype(BF16)
        edge = jnp.concatenate([cot[16 * m : 16 * m + 16, first:last] for m in range(4)], axis=1)
        high, low = split(edge)
        out_ref[16, 0:16, :] = high
        out_ref[16, 16:32, :] = low


def widen_kernel(own_ref, cot_ref, from_left_ref, from_right_ref, upper_ref, lower_ref):
    cot = cot_ref[...]
    for m in range(4):
        out_ref = (upper_ref, lower_ref)[m // 2]
        lanes = slice(HALO * m, HALO * m + HALO)
        base = 16 * (m % 2)
        for q in range(16):
            out_ref[base + q] = jnp.concatenate(
                [
                    own_ref[16 * m + q].astype(F32),
                    from_right_ref[q].astype(F32)[:, lanes],
                    from_left_ref[q].astype(F32)[:, lanes],
                ],
                axis=1,
            ).astype(BF16)
        high, low = split(cot[16 * m : 16 * m + 16, :])
        for part, row, at in ((high, 32, 0), (low, 33, 16)):
            out_ref[row, base : base + 16, :] = jnp.concatenate(
                [
                    part.astype(F32),
                    from_right_ref[16, at : at + 16, :].astype(F32)[:, lanes],
                    from_left_ref[16, at : at + 16, :].astype(F32)[:, lanes],
                ],
                axis=1,
            ).astype(BF16)


def mixed_kernel(place_ref, feat_ref, w_left_ref, w_right_ref, w_in_ref, mixed_ref, rows_ref, cols_ref, picked_ref):
    row = place_ref[0]
    col = place_ref[1]
    row_chunks = [jnp.maximum(2 * row - 1, 0), 2 * row, 2 * row + 1, jnp.minimum(2 * row + 2, 31)]
    col_chunks = [2 * col, 2 * col + 1, jnp.minimum(2 * col + 2, 31), jnp.maximum(2 * col - 1, 0)]
    for chunks, weight_ref, out_ref in (
        (row_chunks, w_left_ref, rows_ref),
        (col_chunks, w_right_ref, cols_ref),
    ):
        for n, chunk in enumerate(chunks):
            for m in range(8):
                at = HALO * n + 4 * m
                picked_ref[at : at + 4, :] = feat_ref[8 * chunk + m].astype(F32)
        out_ref[...] = jnp.dot(
            picked_ref[...].astype(BF16), weight_ref[...], preferred_element_type=F32
        )
    w_in = w_in_ref[...]

    def body(step, carry):
        cols = cols_ref[...]
        rows = rows_ref[pl.ds(ROWS * step, ROWS), :]
        for k in range(0, ROWS, 2):
            pair = [gelu(rows[k + i : k + i + 1, :] + cols).astype(BF16) for i in range(2)]
            out = lax.dot_general(
                w_in, jnp.concatenate(pair, 0), (((1,), (1,)), ((), ())), preferred_element_type=F32
            )
            for i in range(2):
                mixed_ref[ROWS * step + k + i] = out[:, WIDE * i : WIDE * i + WIDE]
        return carry

    lax.fori_loop(0, WIDE // ROWS, body, 0)


def lane_mask(col):
    lane = lax.broadcasted_iota(jnp.int32, (1, WIDE), 1)
    bin_at = TILE * col + jnp.where(lane < TILE + HALO, lane, lane - WIDE)
    return jnp.where((bin_at >= 0) & (bin_at < 1024), 1.0, 0.0).astype(F32)


def many_taps(z_ref, base, rows, rate):
    return (
        z_ref[pl.ds(base - rate, rows), 0:CH, :]
        + z_ref[pl.ds(base, rows), CH : 2 * CH, :]
        + z_ref[pl.ds(base + rate, rows), 2 * CH : 3 * CH, :]
    )


def shifted_rows(value, rate):
    return jnp.concatenate(
        [pltpu.roll(value, rate, 2), value, pltpu.roll(value, WIDE - rate, 2)], axis=1
    ).astype(BF16)


def rows_mask(inside, row, base, rows):
    at = TILE * row - HALO + base + lax.broadcasted_iota(jnp.int32, (rows, 1, 1), 0)
    return jnp.where((at >= 0) & (at < 1024), 1.0, 0.0).astype(F32) * inside[None]


def multiply(weight, patch_ref, z_ref, base, rows):
    for k in range(rows // 2):
        i = base + 2 * k
        pair = jnp.concatenate([patch_ref[i], patch_ref[i + 1]], axis=1)
        z = jnp.dot(weight, pair, preferred_element_type=F32)
        z_ref[i] = z[:, :WIDE]
        z_ref[i + 1] = z[:, WIDE:]


def pipelined(first, last, rows, make, use):
    make(first)

    def body(step, carry):
        base = first + rows * step
        use(base - rows)
        make(base)
        return carry

    lax.fori_loop(1, (last - first) // rows, body, 0)
    use(last - rows)


def main_kernel(
    place_ref,
    mixed_ref,
    part0_ref,
    part1_ref,
    part2_ref,
    part3_ref,
    mirror_ref,
    forward_ref,
    backward_ref,
    w_out_ref,
    direct_ref,
    terms_ref,
    grad_ref,
    round_ref,
    slope0_ref,
    state_ref,
    slope1_ref,
    slope2_ref,
    za_ref,
    zb_ref,
    patch0_ref,
    patch1_ref,
    patch2_ref,
    masked_ref,
    patchb_ref,
    upstream_ref,
    grad2_ref,
):
    row = place_ref[0]
    col = place_ref[1]
    rates = [place_ref[2], place_ref[3], place_ref[4]]
    inside = lane_mask(col)
    patch_refs = (patch0_ref, patch1_ref, patch2_ref)
    parts = (part0_ref, part1_ref, part2_ref, part3_ref)
    w_out = w_out_ref[...]
    z_refs = (za_ref, zb_ref)

    for n in range(4):

        def start(q, carry, n=n):
            given = parts[n][q].astype(F32)
            state_ref[HALO * n + q] = (mixed_ref[HALO * n + q] + given).astype(BF16)
            return carry

        lax.fori_loop(0, HALO, start, 0, unroll=4)

    for layer in range(3):
        z_now = z_refs[layer % 2]
        z_last = z_refs[(layer + 1) % 2]
        slope_ref = (slope0_ref, slope1_ref, slope2_ref)[layer]

        def make(base, layer=layer, z_last=z_last, slope_ref=slope_ref):
            block = pl.ds(base, ROWS)
            state = state_ref[block].astype(F32)
            if layer > 0:
                new = (state + many_taps(z_last, base, ROWS, rates[layer - 1])).astype(BF16)
                state_ref[block] = new
                state = new.astype(F32)
            act, slope = gelu_pair(state)
            slope_ref[block] = slope
            act = act * rows_mask(inside, row, base, ROWS)
            patch_refs[layer][block] = shifted_rows(act, rates[layer])

        def use(base, layer=layer, z_now=z_now):
            multiply(forward_ref[layer], patch_refs[layer], z_now, base, ROWS)

        pipelined(8 * layer, WIDE - 8 * layer, ROWS, make, use)

    def finish(step, carry):
        base = HALO + ROWS * step
        new = state_ref[pl.ds(base, ROWS)].astype(F32) + many_taps(za_ref, base, ROWS, rates[2])
        new = new.astype(BF16).astype(F32)
        direct_ref[pl.ds(base - HALO, ROWS), :] = jnp.sum(new * w_out[None], axis=1)[:, :TILE]
        return carry

    lax.fori_loop(0, TILE // ROWS, finish, 0)

    other = mirror_ref[...].T
    other = jnp.concatenate([other[96:128], other[0:96]], axis=0)
    other = jnp.concatenate([other[:, 32:128], other[:, 0:32]], axis=1)
    for n in range(4):
        mine = parts[n][32].astype(F32) + parts[n][33].astype(F32)
        rows = slice(HALO * n, HALO * n + HALO)
        upstream_ref[rows, :] = 0.5 * (mine + other[rows, :])

    tile_lanes = jnp.where(lax.broadcasted_iota(jnp.int32, (1, WIDE), 1) < TILE, 1.0, 0.0).astype(F32)
    terms_ref[...] = jnp.zeros_like(terms_ref)
    masked_ref[...] = jnp.zeros_like(masked_ref)

    def weight_terms(layer):
        def keep(step, carry):
            block = pl.ds(HALO + 8 * step, 8)
            masked_ref[block] = (round_ref[block].astype(F32) * tile_lanes[None]).astype(BF16)
            return carry

        lax.fori_loop(0, TILE // 8, keep, 0)
        rate = rates[layer]

        def body(step, total):
            base = 24 + 8 * step
            for part in range(2):
                at = base + 4 * part
                left = jnp.concatenate(
                    [
                        jnp.concatenate([masked_ref[at + k + off] for k in range(4)], axis=1)
                        for off in (rate, 0, -rate)
                    ],
                    axis=0,
                )
                right = jnp.concatenate([patch_refs[layer][at + k] for k in range(4)], axis=1)
                total = total + lax.dot_general(
                    left, right, (((1,), (1,)), ((), ())), preferred_element_type=F32
                )
            return total

        terms_ref[layer] = lax.fori_loop(0, 10, body, jnp.zeros((96, 96), F32))

    def back(layer, first, last, one_grad, z_now):
        def make(base):
            rounded = one_grad(base).astype(BF16)
            round_ref[pl.ds(base, ROWS)] = rounded
            patchb_ref[pl.ds(base, ROWS)] = shifted_rows(rounded.astype(F32), rates[layer])

        def use(base):
            multiply(backward_ref[layer], patchb_ref, z_now, base, ROWS)

        pipelined(first, last, ROWS, make, use)
        weight_terms(layer)

    def first_grad(base):
        return upstream_ref[pl.ds(base, ROWS), :][:, None, :] * w_out[None]

    def second_grad(base):
        block = pl.ds(base, ROWS)
        new = first_grad(base) + many_taps(zb_ref, base, ROWS, rates[2]) * slope2_ref[block]
        new = new * rows_mask(inside, row, base, ROWS)
        grad2_ref[block] = new
        return new

    back(2, 8, 120, first_grad, zb_ref)
    back(1, 16, 112, second_grad, za_ref)

    def third_grad(step, carry):
        base = 24 + ROWS * step
        block = pl.ds(base, ROWS)
        new = grad2_ref[block] + many_taps(za_ref, base, ROWS, rates[1]) * slope1_ref[block]
        new = new * rows_mask(inside, row, base, ROWS)
        grad_ref[block] = new
        round_ref[block] = new.astype(BF16)
        return carry

    lax.fori_loop(0, 80 // ROWS, third_grad, 0)
    weight_terms(0)


def last_kernel(
    place_ref,
    grad_ref,
    round_ref,
    slope0_ref,
    rows_ref,
    cols_ref,
    backward_ref,
    w_in_ref,
    row_ref,
    col_ref,
    z_ref,
    patch_ref,
):
    rate = place_ref[2]

    def make(base):
        patch_ref[pl.ds(base, ROWS)] = shifted_rows(round_ref[pl.ds(base, ROWS)].astype(F32), rate)

    def use(base):
        multiply(backward_ref[0], patch_ref, z_ref, base, ROWS)

    pipelined(24, 104, ROWS, make, use)
    w_in = w_in_ref[...]
    cols = cols_ref[0:TILE, :]

    def body(step, total):
        base = HALO + ROWS * step
        block = pl.ds(base, ROWS)
        start = grad_ref[block] + many_taps(z_ref, base, ROWS, rate) * slope0_ref[block]
        start = start[:, :, :TILE].astype(BF16)
        rows = rows_ref[block, :]
        sums = []
        for k in range(ROWS):
            hidden = lax.dot_general(
                start[k], w_in, (((0,), (0,)), ((), ())), preferred_element_type=F32
            )
            outer = hidden * gelu_pair(rows[k : k + 1, :] + cols)[1]
            sums.append(jnp.sum(outer, axis=0, keepdims=True))
            total = total + outer
        row_ref[pl.ds(base - HALO, ROWS), :] = jnp.concatenate(sums, axis=0).astype(BF16)
        return total

    total = lax.fori_loop(0, TILE // ROWS, body, jnp.zeros((TILE, 128), F32))
    col_ref[...] = total.astype(BF16)


def shape(*dims, dtype=F32):
    return jax.ShapeDtypeStruct(dims, dtype)


def call(kernel, outs, specs, scratch=(), mib=8, cost=1):
    return pl.pallas_call(
        kernel,
        out_shape=outs,
        in_specs=specs,
        out_specs=[VMEM] * len(outs),
        scratch_shapes=list(scratch),
        compiler_params=pltpu.CompilerParams(vmem_limit_bytes=mib * 2**20),
        cost_estimate=pl.CostEstimate(
            flops=cost * 10**9, bytes_accessed=cost * 3 * 10**6, transcendentals=0
        ),
    )


def flips(axis, bit):
    return [(i, i ^ bit) for i in range(lax.axis_size(axis))]


def on_device(features, w_left, w_right, w_in, pair_input, conv_w, w_out, dilation, cotangent):
    n_row = lax.axis_size("row")
    n_col = lax.axis_size("col")
    row_at = lax.axis_index("row").astype(jnp.int32)
    col_at = lax.axis_index("col").astype(jnp.int32)
    place = jnp.concatenate([jnp.stack([row_at, col_at]), dilation, jnp.zeros((3,), jnp.int32)])
    up = [(i, i + 1) for i in range(n_row - 1)]
    down = [(i + 1, i) for i in range(n_row - 1)]
    swap = [(r * n_col + c, c * n_col + r) for r in range(n_row) for c in range(n_col)]

    own, left_edge, right_edge = call(
        edges_kernel,
        [shape(TILE, CH, TILE, dtype=BF16)] + [shape(17, CH, WIDE, dtype=BF16)] * 2,
        [VMEM] * 2,
    )(pair_input, cotangent)
    from_left = lax.ppermute(right_edge, "col", up)
    from_right = lax.ppermute(left_edge, "col", down)

    sent = jnp.broadcast_to(features[None], (n_row * n_col,) + features.shape)
    gathered = lax.all_to_all(sent, ("row", "col"), 0, 0)
    from_left, from_right, gathered = lax.optimization_barrier((from_left, from_right, gathered))

    upper, lower = call(
        widen_kernel, [shape(HALO + 2, CH, WIDE, dtype=BF16)] * 2, [VMEM] * 4
    )(own, cotangent, from_left, from_right)
    above = lax.ppermute(lower, "row", up)
    below = lax.ppermute(upper, "row", down)

    mixed, row_project, col_project = call(
        mixed_kernel,
        [shape(WIDE, CH, WIDE), shape(WIDE, 128), shape(WIDE, 128)],
        [SMEM] + [VMEM] * 4,
        [pltpu.VMEM((WIDE, 128), F32)],
        16,
        6,
    )(place, gathered, w_left, w_right, w_in)

    wide_cot = jnp.concatenate(
        [part[32].astype(F32) + part[33].astype(F32) for part in (above, upper, lower, below)], axis=0
    )
    mirrored = lax.ppermute(wide_cot, ("row", "col"), swap)

    forward_w = conv_w.reshape(3, CH, 3, 3 * CH).transpose(0, 2, 1, 3).reshape(3, 96, 96)
    backward_w = (
        conv_w.reshape(3, CH, 3, 3, CH)[:, :, ::-1, ::-1, :].transpose(0, 2, 4, 3, 1).reshape(3, 96, 96)
    )
    w_out_wide = jnp.broadcast_to(w_out.astype(F32)[:, None], (CH, WIDE))
    big = (WIDE, CH, WIDE)
    direct, terms, grad, rounded, slope0 = call(
        main_kernel,
        [shape(TILE, TILE), shape(3, 96, 96), shape(*big), shape(*big, dtype=BF16), shape(*big)],
        [SMEM] + [VMEM] * 9,
        [
            pltpu.VMEM(big, BF16),
            pltpu.VMEM(big, F32),
            pltpu.VMEM(big, F32),
            pltpu.VMEM((WIDE, 96, WIDE), F32),
            pltpu.VMEM((WIDE, 96, WIDE), F32),
            pltpu.VMEM((WIDE, 96, WIDE), BF16),
            pltpu.VMEM((WIDE, 96, WIDE), BF16),
            pltpu.VMEM((WIDE, 96, WIDE), BF16),
            pltpu.VMEM(big, BF16),
            pltpu.VMEM((WIDE, 96, WIDE), BF16),
            pltpu.VMEM((WIDE, WIDE), F32),
            pltpu.VMEM(big, F32),
        ],
        40,
        24,
    )(place, mixed, above, upper, lower, below, mirrored, forward_w, backward_w, w_out_wide)

    def summed(value, axis, bit):
        other = lax.ppermute(value, axis, flips(axis, bit))
        return (value.astype(F32) + other.astype(F32)).astype(BF16)

    direct_other = lax.ppermute(direct, ("row", "col"), swap)
    packed = summed(terms.astype(BF16).reshape(216, 128), "row", 1)
    grad, packed = lax.optimization_barrier((grad, packed))
    packed = summed(packed, "row", 2)

    row_part, col_part = call(
        last_kernel,
        [shape(TILE, 128, dtype=BF16), shape(TILE, 128, dtype=BF16)],
        [SMEM] + [VMEM] * 7,
        [pltpu.VMEM((WIDE, 96, WIDE), F32), pltpu.VMEM((WIDE, 96, WIDE), BF16)],
        24,
        7,
    )(place, grad, rounded, slope0, row_project, col_project, backward_w, w_in)

    logits = 0.5 * (direct + direct_other.T)
    packed = jnp.concatenate([col_part, packed], axis=0)
    for bit in (4, 8):
        packed = summed(packed, "row", bit)
    col_part = packed[:TILE]
    packed = jnp.concatenate([row_part, packed[TILE:]], axis=0)
    for bit in (1, 2):
        packed = summed(packed, "col", bit)
        col_part = summed(col_part, "row", bit)
    for bit in (4, 8):
        packed = summed(packed, "col", bit)
    row_part = packed[:TILE]
    conv_grads = (
        packed[TILE:].reshape(3, 3, CH, 96).transpose(0, 2, 1, 3).reshape(3, CH, 288).astype(F32)
        / (TILE * n_row)
    )
    row_part = row_part.astype(F32)
    col_part = col_part.astype(F32)
    grad_rows = jnp.dot(row_part, w_left.astype(F32).T, precision=lax.Precision.HIGHEST)
    grad_cols = jnp.dot(col_part, w_right.astype(F32).T, precision=lax.Precision.HIGHEST)
    return (logits, grad_rows, grad_cols, conv_grads)


def solution(mesh):
    return jax.shard_map(
        on_device,
        mesh=mesh,
        in_specs=(
            P(("row", "col"), None),
            P(),
            P(),
            P(),
            P(None, "row", "col"),
            P(),
            P(),
            P(),
            P("row", "col"),
        ),
        out_specs=(P("row", "col"), P("row", None), P("col", None), P()),
        check_vma=False,
    )
```

```python
import jax
import jax.numpy as jnp
from jax import lax
from jax.experimental import pallas as pl
from jax.experimental.pallas import tpu as pltpu
from jax.sharding import PartitionSpec as P

F32 = jnp.float32
BF16 = jnp.bfloat16
K_ROOT = 0.7978845608028654
CUBIC = 0.044715
TILE = 64
HALO = 32
WIDE = TILE + 2 * HALO
CH = 32
ROWS = 16
VMEM = pl.BlockSpec(memory_space=pltpu.VMEM)
SMEM = pl.BlockSpec(memory_space=pltpu.SMEM)


def gelu(value):
    inner = value * (K_ROOT + (K_ROOT * CUBIC) * (value * value))
    half = 0.5 * value
    return half + half * jnp.tanh(inner)


def gelu_pair(value):
    square = value * value
    tangent = jnp.tanh(value * (K_ROOT + (K_ROOT * CUBIC) * square))
    half = 0.5 * value
    up = 0.5 + 0.5 * tangent
    result = value * up
    slope = up + half * (1.0 - tangent * tangent) * (K_ROOT + (3.0 * K_ROOT * CUBIC) * square)
    return result, slope


def split(value):
    high = value.astype(BF16)
    return high, (value - high.astype(F32)).astype(BF16)


def edges_kernel(pair_ref, cot_ref, feat_ref, own_ref, left_ref, right_ref, sent_ref):
    sent_ref[...] = jnp.broadcast_to(feat_ref[...][None], sent_ref.shape)
    own = jnp.swapaxes(pair_ref[...].astype(F32), 0, 1)
    own_ref[...] = own.astype(BF16)
    cot = cot_ref[...]
    for out_ref, first in ((left_ref, 0), (right_ref, TILE - HALO)):
        last = first + HALO
        for q in range(16):
            out_ref[q] = jnp.concatenate(
                [own[q + 16 * m, :, first:last] for m in range(4)], axis=1
            ).astype(BF16)
        edge = jnp.concatenate([cot[16 * m : 16 * m + 16, first:last] for m in range(4)], axis=1)
        high, low = split(edge)
        out_ref[16, 0:16, :] = high
        out_ref[16, 16:32, :] = low


def widen_kernel(own_ref, cot_ref, from_left_ref, from_right_ref, upper_ref, lower_ref):
    cot = cot_ref[...]
    for m in range(4):
        out_ref = (upper_ref, lower_ref)[m // 2]
        lanes = slice(HALO * m, HALO * m + HALO)
        base = 16 * (m % 2)
        for q in range(16):
            out_ref[base + q] = jnp.concatenate(
                [
                    own_ref[16 * m + q].astype(F32),
                    from_right_ref[q].astype(F32)[:, lanes],
                    from_left_ref[q].astype(F32)[:, lanes],
                ],
                axis=1,
            ).astype(BF16)
        high, low = split(cot[16 * m : 16 * m + 16, :])
        for part, row, at in ((high, 32, 0), (low, 33, 16)):
            out_ref[row, base : base + 16, :] = jnp.concatenate(
                [
                    part.astype(F32),
                    from_right_ref[16, at : at + 16, :].astype(F32)[:, lanes],
                    from_left_ref[16, at : at + 16, :].astype(F32)[:, lanes],
                ],
                axis=1,
            ).astype(BF16)


def mixed_kernel(place_ref, feat_ref, w_left_ref, w_right_ref, w_in_ref, mixed_ref, rows_ref, cols_ref, picked_ref):
    row = place_ref[0]
    col = place_ref[1]
    row_chunks = [jnp.maximum(2 * row - 1, 0), 2 * row, 2 * row + 1, jnp.minimum(2 * row + 2, 31)]
    col_chunks = [2 * col, 2 * col + 1, jnp.minimum(2 * col + 2, 31), jnp.maximum(2 * col - 1, 0)]
    for chunks, weight_ref, out_ref in (
        (row_chunks, w_left_ref, rows_ref),
        (col_chunks, w_right_ref, cols_ref),
    ):
        for n, chunk in enumerate(chunks):
            for m in range(8):
                at = HALO * n + 4 * m
                picked_ref[at : at + 4, :] = feat_ref[8 * chunk + m].astype(F32)
        out_ref[...] = jnp.dot(
            picked_ref[...].astype(BF16), weight_ref[...], preferred_element_type=F32
        )
    w_in = w_in_ref[...]

    def body(step, carry):
        cols = cols_ref[...]
        rows = rows_ref[pl.ds(ROWS * step, ROWS), :]
        for k in range(0, ROWS, 2):
            pair = [gelu(rows[k + i : k + i + 1, :] + cols).astype(BF16) for i in range(2)]
            out = lax.dot_general(
                w_in, jnp.concatenate(pair, 0), (((1,), (1,)), ((), ())), preferred_element_type=F32
            )
            for i in range(2):
                mixed_ref[ROWS * step + k + i] = out[:, WIDE * i : WIDE * i + WIDE]
        return carry

    lax.fori_loop(0, WIDE // ROWS, body, 0)


def lane_mask(col):
    lane = lax.broadcasted_iota(jnp.int32, (1, WIDE), 1)
    bin_at = TILE * col + jnp.where(lane < TILE + HALO, lane, lane - WIDE)
    return jnp.where((bin_at >= 0) & (bin_at < 1024), 1.0, 0.0).astype(F32)


def many_taps(z_ref, base, rows, rate):
    return (
        z_ref[pl.ds(base - rate, rows), 0:CH, :]
        + z_ref[pl.ds(base, rows), CH : 2 * CH, :]
        + z_ref[pl.ds(base + rate, rows), 2 * CH : 3 * CH, :]
    )


def shifted_rows(value, rate):
    return jnp.concatenate(
        [pltpu.roll(value, rate, 2), value, pltpu.roll(value, WIDE - rate, 2)], axis=1
    ).astype(BF16)


def rows_mask(inside, row, base, rows):
    at = TILE * row - HALO + base + lax.broadcasted_iota(jnp.int32, (rows, 1, 1), 0)
    return jnp.where((at >= 0) & (at < 1024), 1.0, 0.0).astype(F32) * inside[None]


def multiply(weight, patch_ref, z_ref, base, rows):
    for k in range(rows // 2):
        i = base + 2 * k
        pair = jnp.concatenate([patch_ref[i], patch_ref[i + 1]], axis=1)
        z = jnp.dot(weight, pair, preferred_element_type=F32)
        z_ref[i] = z[:, :WIDE]
        z_ref[i + 1] = z[:, WIDE:]


def pipelined(first, last, rows, make, use):
    make(first)

    def body(step, carry):
        base = first + rows * step
        use(base - rows)
        make(base)
        return carry

    lax.fori_loop(1, (last - first) // rows, body, 0)
    use(last - rows)


def main_kernel(
    place_ref,
    mixed_ref,
    part0_ref,
    part1_ref,
    part2_ref,
    part3_ref,
    mirror_ref,
    forward_ref,
    backward_ref,
    w_out_ref,
    direct_ref,
    terms_ref,
    grad_ref,
    last_ref,
    round_ref,
    slope0_ref,
    state_ref,
    slope1_ref,
    slope2_ref,
    za_ref,
    zb_ref,
    patch0_ref,
    patch1_ref,
    patch2_ref,
    masked_ref,
    patchb_ref,
    upstream_ref,
    grad2_ref,
):
    row = place_ref[0]
    col = place_ref[1]
    rates = [place_ref[2], place_ref[3], place_ref[4]]
    inside = lane_mask(col)
    patch_refs = (patch0_ref, patch1_ref, patch2_ref)
    parts = (part0_ref, part1_ref, part2_ref, part3_ref)
    w_out = w_out_ref[...]
    z_refs = (za_ref, zb_ref)

    for n in range(4):

        def start(q, carry, n=n):
            given = parts[n][q].astype(F32)
            state_ref[HALO * n + q] = (mixed_ref[HALO * n + q] + given).astype(BF16)
            return carry

        lax.fori_loop(0, HALO, start, 0, unroll=4)

    for layer in range(3):
        z_now = z_refs[layer % 2]
        z_last = z_refs[(layer + 1) % 2]
        slope_ref = (slope0_ref, slope1_ref, slope2_ref)[layer]

        def make(base, layer=layer, z_last=z_last, slope_ref=slope_ref):
            block = pl.ds(base, ROWS)
            state = state_ref[block].astype(F32)
            if layer > 0:
                new = (state + many_taps(z_last, base, ROWS, rates[layer - 1])).astype(BF16)
                state_ref[block] = new
                state = new.astype(F32)
            act, slope = gelu_pair(state)
            slope_ref[block] = slope
            act = act * rows_mask(inside, row, base, ROWS)
            patch_refs[layer][block] = shifted_rows(act, rates[layer])

        def use(base, layer=layer, z_now=z_now):
            multiply(forward_ref[layer], patch_refs[layer], z_now, base, ROWS)

        pipelined(8 * layer, WIDE - 8 * layer, ROWS, make, use)

    def finish(step, carry):
        base = HALO + ROWS * step
        new = state_ref[pl.ds(base, ROWS)].astype(F32) + many_taps(za_ref, base, ROWS, rates[2])
        new = new.astype(BF16).astype(F32)
        direct_ref[pl.ds(base - HALO, ROWS), :] = jnp.sum(new * w_out[None], axis=1)[:, :TILE]
        return carry

    lax.fori_loop(0, TILE // ROWS, finish, 0)

    other = mirror_ref[...].T
    other = jnp.concatenate([other[96:128], other[0:96]], axis=0)
    other = jnp.concatenate([other[:, 32:128], other[:, 0:32]], axis=1)
    for n in range(4):
        mine = parts[n][32].astype(F32) + parts[n][33].astype(F32)
        rows = slice(HALO * n, HALO * n + HALO)
        upstream_ref[rows, :] = 0.5 * (mine + other[rows, :])

    tile_lanes = jnp.where(lax.broadcasted_iota(jnp.int32, (1, WIDE), 1) < TILE, 1.0, 0.0).astype(F32)
    masked_ref[...] = jnp.zeros_like(masked_ref)

    def weight_terms(layer):
        def keep(step, carry):
            block = pl.ds(HALO + 8 * step, 8)
            masked_ref[block] = (round_ref[block].astype(F32) * tile_lanes[None]).astype(BF16)
            return carry

        lax.fori_loop(0, TILE // 8, keep, 0)
        rate = rates[layer]

        def body(step, total):
            base = 24 + 8 * step
            for part in range(2):
                at = base + 4 * part
                left = jnp.concatenate(
                    [
                        jnp.concatenate([masked_ref[at + k + off] for k in range(4)], axis=1)
                        for off in (rate, 0, -rate)
                    ],
                    axis=0,
                )
                right = jnp.concatenate([patch_refs[layer][at + k] for k in range(4)], axis=1)
                total = total + lax.dot_general(
                    left, right, (((1,), (1,)), ((), ())), preferred_element_type=F32
                )
            return total

        return lax.fori_loop(0, 10, body, jnp.zeros((96, 96), F32))

    def back(layer, first, last, one_grad, z_now):
        def make(base):
            rounded = one_grad(base).astype(BF16)
            round_ref[pl.ds(base, ROWS)] = rounded
            patchb_ref[pl.ds(base, ROWS)] = shifted_rows(rounded.astype(F32), rates[layer])

        def use(base):
            multiply(backward_ref[layer], patchb_ref, z_now, base, ROWS)

        pipelined(first, last, ROWS, make, use)
        return weight_terms(layer)

    def first_grad(base):
        return upstream_ref[pl.ds(base, ROWS), :][:, None, :] * w_out[None]

    def second_grad(base):
        block = pl.ds(base, ROWS)
        new = first_grad(base) + many_taps(zb_ref, base, ROWS, rates[2]) * slope2_ref[block]
        new = new * rows_mask(inside, row, base, ROWS)
        grad2_ref[block] = new
        return new

    terms2 = back(2, 8, 120, first_grad, zb_ref)
    terms1 = back(1, 16, 112, second_grad, za_ref)

    def third_grad(step, carry):
        base = 24 + ROWS * step
        block = pl.ds(base, ROWS)
        new = grad2_ref[block] + many_taps(za_ref, base, ROWS, rates[1]) * slope1_ref[block]
        new = new * rows_mask(inside, row, base, ROWS)
        rounded = new.astype(BF16)
        last_ref[pl.ds(base - 24, ROWS)] = rounded
        round_ref[block] = rounded
        slope = pltpu.roll(slope0_ref[block], TILE, 2)
        grad_ref[pl.ds(base - 24, ROWS)] = jnp.where(first_half, new, slope)
        return carry

    first_half = lax.broadcasted_iota(jnp.int32, (1, 1, WIDE), 2) < TILE
    lax.fori_loop(0, 80 // ROWS, third_grad, 0)
    terms0 = weight_terms(0)
    terms = jnp.concatenate([terms0, terms1, terms2], axis=0)
    spare = jnp.concatenate([terms[216:288, 32 * k : 32 * k + 32] for k in range(3)], axis=0)
    terms_ref[...] = jnp.concatenate([terms[0:216], spare], axis=1).astype(BF16)


def last_kernel(
    place_ref,
    grad_ref,
    round_ref,
    rows_ref,
    cols_ref,
    backward_ref,
    w_in_ref,
    row_ref,
    col_ref,
    z_ref,
    patch_ref,
):
    rate = place_ref[2]

    def make(base):
        patch_ref[pl.ds(base, ROWS)] = shifted_rows(round_ref[pl.ds(base, ROWS)].astype(F32), rate)

    def use(base):
        multiply(backward_ref[0], patch_ref, z_ref, base, ROWS)

    pipelined(0, 80, ROWS, make, use)
    w_in = w_in_ref[...]
    cols = cols_ref[0:TILE, :]

    def body(step, total):
        base = ROWS * step
        both = grad_ref[pl.ds(base + 8, ROWS)]
        slope = pltpu.roll(both, TILE, 2)
        start = both + many_taps(z_ref, base + 8, ROWS, rate) * slope
        start = start[:, :, :TILE].astype(BF16)
        rows = rows_ref[pl.ds(base + HALO, ROWS), :]
        sums = []
        for k in range(ROWS):
            hidden = lax.dot_general(
                start[k], w_in, (((0,), (0,)), ((), ())), preferred_element_type=F32
            )
            outer = hidden * gelu_pair(rows[k : k + 1, :] + cols)[1]
            sums.append(jnp.sum(outer, axis=0, keepdims=True))
            total = total + outer
        row_ref[pl.ds(base, ROWS), :] = jnp.concatenate(sums, axis=0).astype(BF16)
        return total

    total = lax.fori_loop(0, TILE // ROWS, body, jnp.zeros((TILE, 128), F32))
    col_ref[...] = total.astype(BF16)


def finish_kernel(
    mine_ref,
    got_ref,
    col_ref,
    w_left_ref,
    w_right_ref,
    direct_ref,
    other_ref,
    logits_ref,
    grad_rows_ref,
    grad_cols_ref,
    conv_ref,
):
    logits_ref[...] = 0.5 * (direct_ref[...] + other_ref[...].T)
    total = mine_ref[...].astype(F32) + got_ref[...].astype(F32)
    for value, weight_ref, out_ref in (
        (total[0:TILE], w_left_ref, grad_rows_ref),
        (col_ref[...].astype(F32), w_right_ref, grad_cols_ref),
    ):
        out_ref[...] = lax.dot_general(
            value,
            weight_ref[...].astype(F32),
            (((1,), (1,)), ((), ())),
            precision=lax.Precision.HIGHEST,
            preferred_element_type=F32,
        )
    terms = total[TILE:] * (1.0 / 1024.0)
    spare = jnp.concatenate([terms[72 * k : 72 * k + 72, 96:128] for k in range(3)], axis=1)
    terms = jnp.concatenate([terms[:, 0:96], spare], axis=0)
    for layer in range(3):
        at = 96 * layer
        conv_ref[layer] = jnp.concatenate(
            [terms[at + CH * a : at + CH * a + CH] for a in range(3)], axis=1
        )


def shape(*dims, dtype=F32):
    return jax.ShapeDtypeStruct(dims, dtype)


def call(kernel, outs, specs, scratch=(), mib=8, cost=1):
    return pl.pallas_call(
        kernel,
        out_shape=outs,
        in_specs=specs,
        out_specs=[VMEM] * len(outs),
        scratch_shapes=list(scratch),
        compiler_params=pltpu.CompilerParams(vmem_limit_bytes=mib * 2**20),
        cost_estimate=pl.CostEstimate(
            flops=cost * 10**9, bytes_accessed=cost * 3 * 10**6, transcendentals=0
        ),
    )


def on_device(features, w_left, w_right, w_in, pair_input, conv_w, w_out, dilation, cotangent):
    n_row = lax.axis_size("row")
    n_col = lax.axis_size("col")
    row_at = lax.axis_index("row").astype(jnp.int32)
    col_at = lax.axis_index("col").astype(jnp.int32)
    place = jnp.concatenate([jnp.stack([row_at, col_at]), dilation, jnp.zeros((3,), jnp.int32)])
    up = [(i, i + 1) for i in range(n_row - 1)]
    down = [(i + 1, i) for i in range(n_row - 1)]
    swap = [(r * n_col + c, c * n_col + r) for r in range(n_row) for c in range(n_col)]

    own, left_edge, right_edge, sent = call(
        edges_kernel,
        [shape(TILE, CH, TILE, dtype=BF16)]
        + [shape(17, CH, WIDE, dtype=BF16)] * 2
        + [shape(n_row * n_col, *features.shape, dtype=BF16)],
        [VMEM] * 3,
    )(pair_input, cotangent, features)
    from_left = lax.ppermute(right_edge, "col", up)
    from_right = lax.ppermute(left_edge, "col", down)
    gathered = lax.all_to_all(sent, ("row", "col"), 0, 0)
    from_left, from_right, gathered = lax.optimization_barrier((from_left, from_right, gathered))

    upper, lower = call(
        widen_kernel, [shape(HALO + 2, CH, WIDE, dtype=BF16)] * 2, [VMEM] * 4
    )(own, cotangent, from_left, from_right)
    above = lax.ppermute(lower, "row", up)
    below = lax.ppermute(upper, "row", down)

    mixed, row_project, col_project = call(
        mixed_kernel,
        [shape(WIDE, CH, WIDE), shape(WIDE, 128), shape(WIDE, 128)],
        [SMEM] + [VMEM] * 4,
        [pltpu.VMEM((WIDE, 128), F32)],
        16,
        6,
    )(place, gathered, w_left, w_right, w_in)

    wide_cot = jnp.concatenate(
        [part[32].astype(F32) + part[33].astype(F32) for part in (above, upper, lower, below)], axis=0
    )
    mirrored = lax.ppermute(wide_cot, ("row", "col"), swap)

    forward_w = conv_w.reshape(3, CH, 3, 3 * CH).transpose(0, 2, 1, 3).reshape(3, 96, 96)
    backward_w = (
        conv_w.reshape(3, CH, 3, 3, CH)[:, :, ::-1, ::-1, :].transpose(0, 2, 4, 3, 1).reshape(3, 96, 96)
    )
    w_out_wide = jnp.broadcast_to(w_out.astype(F32)[:, None], (CH, WIDE))
    big = (WIDE, CH, WIDE)
    direct, terms, grad, rounded = call(
        main_kernel,
        [shape(TILE, TILE), shape(216, 128, dtype=BF16), shape(80, CH, WIDE), shape(80, CH, WIDE, dtype=BF16)],
        [SMEM] + [VMEM] * 9,
        [
            pltpu.VMEM(big, BF16),
            pltpu.VMEM(big, F32),
            pltpu.VMEM(big, BF16),
            pltpu.VMEM(big, F32),
            pltpu.VMEM(big, F32),
            pltpu.VMEM((WIDE, 96, WIDE), F32),
            pltpu.VMEM((WIDE, 96, WIDE), F32),
            pltpu.VMEM((WIDE, 96, WIDE), BF16),
            pltpu.VMEM((WIDE, 96, WIDE), BF16),
            pltpu.VMEM((WIDE, 96, WIDE), BF16),
            pltpu.VMEM(big, BF16),
            pltpu.VMEM((WIDE, 96, WIDE), BF16),
            pltpu.VMEM((WIDE, WIDE), F32),
            pltpu.VMEM(big, F32),
        ],
        42,
        24,
    )(place, mixed, above, upper, lower, below, mirrored, forward_w, backward_w, w_out_wide)

    def flipped(value, row_bits, col_bits):
        pairs = [
            (r * n_col + c, (r ^ row_bits) * n_col + (c ^ col_bits))
            for r in range(n_row)
            for c in range(n_col)
        ]
        return lax.ppermute(value, ("row", "col"), pairs)

    def summed(value, row_bits, col_bits):
        return (value.astype(F32) + flipped(value, row_bits, col_bits).astype(F32)).astype(BF16)

    direct_other = lax.ppermute(direct, ("row", "col"), swap)
    terms = summed(terms, 1, 0)
    grad, rounded, row_project, col_project, terms = lax.optimization_barrier(
        (grad, rounded, row_project, col_project, terms)
    )
    terms = summed(terms, 2, 0)
    row_part, col_part = call(
        last_kernel,
        [shape(TILE, 128, dtype=BF16), shape(TILE, 128, dtype=BF16)],
        [SMEM] + [VMEM] * 6,
        [pltpu.VMEM((80, 96, WIDE), F32), pltpu.VMEM((80, 96, WIDE), BF16)],
        16,
        7,
    )(place, grad, rounded, row_project, col_project, backward_w, w_in)

    packed = jnp.concatenate([col_part, terms], axis=0)
    packed = summed(packed, 4, 0)
    row_part = summed(row_part, 0, 1)
    packed = summed(packed, 12, 0)
    col_part = packed[:TILE]
    terms = summed(packed[TILE:], 2, 1)
    col_part = summed(col_part, 1, 0)
    packed = jnp.concatenate([row_part, terms], axis=0)
    packed = summed(packed, 0, 2)
    col_part = summed(col_part, 2, 0)
    packed = summed(packed, 0, 4)
    return tuple(
        call(
            finish_kernel,
            [shape(TILE, TILE), shape(TILE, 128), shape(TILE, 128), shape(3, CH, 288)],
            [VMEM] * 7,
        )(packed, flipped(packed, 0, 12), col_part, w_left, w_right, direct, direct_other)
    )


def solution(mesh):
    return jax.shard_map(
        on_device,
        mesh=mesh,
        in_specs=(
            P(("row", "col"), None),
            P(),
            P(),
            P(),
            P(None, "row", "col"),
            P(),
            P(),
            P(),
            P("row", "col"),
        ),
        out_specs=(P("row", "col"), P("row", None), P("col", None), P()),
        check_vma=False,
    )
```

```python
import jax
import jax.numpy as jnp
from jax import lax
from jax.experimental import pallas as pl
from jax.experimental.pallas import tpu as pltpu
from jax.sharding import PartitionSpec as P

F32 = jnp.float32
BF16 = jnp.bfloat16
K_ROOT = 0.7978845608028654
CUBIC = 0.044715
TILE = 64
HALO = 32
WIDE = TILE + 2 * HALO
CH = 32
ROWS = 16
VMEM = pl.BlockSpec(memory_space=pltpu.VMEM)
SMEM = pl.BlockSpec(memory_space=pltpu.SMEM)


def gelu(value):
    inner = value * (K_ROOT + (K_ROOT * CUBIC) * (value * value))
    half = 0.5 * value
    return half + half * jnp.tanh(inner)


def gelu_pair(value):
    square = value * value
    tangent = jnp.tanh(value * (K_ROOT + (K_ROOT * CUBIC) * square))
    half = 0.5 * value
    up = 0.5 + 0.5 * tangent
    result = value * up
    slope = up + half * (1.0 - tangent * tangent) * (K_ROOT + (3.0 * K_ROOT * CUBIC) * square)
    return result, slope


def split(value):
    high = value.astype(BF16)
    return high, (value - high.astype(F32)).astype(BF16)


def spread_kernel(feat_ref, sent_ref):
    sent_ref[...] = jnp.broadcast_to(feat_ref[...][None], sent_ref.shape)


def edges_kernel(
    pair_ref, cot_ref, mirror_ref, own_ref, left_ref, right_ref, upstream_ref
):
    own = jnp.swapaxes(pair_ref[...].astype(F32), 0, 1)
    own_ref[...] = own.astype(BF16)
    cot = 0.5 * (cot_ref[...] + mirror_ref[...].T)
    upstream_ref[...] = cot
    for out_ref, first in ((left_ref, 0), (right_ref, TILE - HALO)):
        last = first + HALO
        for q in range(16):
            out_ref[q] = jnp.concatenate(
                [own[q + 16 * m, :, first:last] for m in range(4)], axis=1
            ).astype(BF16)
        edge = jnp.concatenate([cot[16 * m : 16 * m + 16, first:last] for m in range(4)], axis=1)
        high, low = split(edge)
        out_ref[16, 0:16, :] = high
        out_ref[16, 16:32, :] = low


def widen_kernel(own_ref, upstream_ref, from_left_ref, from_right_ref, upper_ref, lower_ref):
    cot = upstream_ref[...]
    for m in range(4):
        out_ref = (upper_ref, lower_ref)[m // 2]
        lanes = slice(HALO * m, HALO * m + HALO)
        base = 16 * (m % 2)
        for q in range(16):
            out_ref[base + q] = jnp.concatenate(
                [
                    own_ref[16 * m + q].astype(F32),
                    from_right_ref[q].astype(F32)[:, lanes],
                    from_left_ref[q].astype(F32)[:, lanes],
                ],
                axis=1,
            ).astype(BF16)
        high, low = split(cot[16 * m : 16 * m + 16, :])
        for part, row, at in ((high, 32, 0), (low, 33, 16)):
            out_ref[row, base : base + 16, :] = jnp.concatenate(
                [
                    part.astype(F32),
                    from_right_ref[16, at : at + 16, :].astype(F32)[:, lanes],
                    from_left_ref[16, at : at + 16, :].astype(F32)[:, lanes],
                ],
                axis=1,
            ).astype(BF16)


def mixed_kernel(
    place_ref, feat_ref, w_left_ref, w_right_ref, w_in_ref, conv_ref,
    mixed_ref, rows_ref, cols_ref, forward_ref, backward_ref, picked_ref,
):
    row = place_ref[0]
    col = place_ref[1]
    row_chunks = [jnp.maximum(2 * row - 1, 0), 2 * row, 2 * row + 1, jnp.minimum(2 * row + 2, 31)]
    col_chunks = [2 * col, 2 * col + 1, jnp.minimum(2 * col + 2, 31), jnp.maximum(2 * col - 1, 0)]
    for chunks, weight_ref, out_ref in (
        (row_chunks, w_left_ref, rows_ref),
        (col_chunks, w_right_ref, cols_ref),
    ):
        for n, chunk in enumerate(chunks):
            for m in range(8):
                at = HALO * n + 4 * m
                picked_ref[at : at + 4, :] = feat_ref[8 * chunk + m].astype(F32)
        out_ref[...] = jnp.dot(
            picked_ref[...].astype(BF16), weight_ref[...], preferred_element_type=F32
        )
    for layer in range(3):
        weight = conv_ref[layer].astype(F32)
        turned = jnp.concatenate([weight, jnp.zeros((CH, 96), F32)], axis=1)
        turned = jnp.concatenate([turned[:, 128 * k : 128 * k + 128].T for k in range(3)], axis=0)
        for a in range(3):
            forward_ref[layer, CH * a : CH * a + CH, :] = weight[:, 96 * a : 96 * a + 96].astype(BF16)
            taps = [8 - 3 * a - b for b in range(3)]
            backward_ref[layer, CH * a : CH * a + CH, :] = jnp.concatenate(
                [turned[CH * tap : CH * tap + CH] for tap in taps], axis=1
            ).astype(BF16)
    w_in = w_in_ref[...]

    def body(step, carry):
        cols = cols_ref[...]
        rows = rows_ref[pl.ds(ROWS * step, ROWS), :]
        for k in range(0, ROWS, 2):
            pair = [gelu(rows[k + i : k + i + 1, :] + cols).astype(BF16) for i in range(2)]
            out = lax.dot_general(
                w_in, jnp.concatenate(pair, 0), (((1,), (1,)), ((), ())), preferred_element_type=F32
            )
            for i in range(2):
                mixed_ref[ROWS * step + k + i] = out[:, WIDE * i : WIDE * i + WIDE]
        return carry

    lax.fori_loop(0, WIDE // ROWS, body, 0)


def lane_mask(col):
    lane = lax.broadcasted_iota(jnp.int32, (1, WIDE), 1)
    bin_at = TILE * col + jnp.where(lane < TILE + HALO, lane, lane - WIDE)
    return jnp.where((bin_at >= 0) & (bin_at < 1024), 1.0, 0.0).astype(F32)


def many_taps(z_ref, base, rows, rate):
    return (
        z_ref[pl.ds(base - rate, rows), 0:CH, :]
        + z_ref[pl.ds(base, rows), CH : 2 * CH, :]
        + z_ref[pl.ds(base + rate, rows), 2 * CH : 3 * CH, :]
    )


def shifted_rows(value, rate):
    return jnp.concatenate(
        [pltpu.roll(value, rate, 2), value, pltpu.roll(value, WIDE - rate, 2)], axis=1
    ).astype(BF16)


def rows_mask(inside, row, base, rows):
    at = TILE * row - HALO + base + lax.broadcasted_iota(jnp.int32, (rows, 1, 1), 0)
    return jnp.where((at >= 0) & (at < 1024), 1.0, 0.0).astype(F32) * inside[None]


def multiply(weight, patch_ref, z_ref, base, rows):
    for k in range(rows // 2):
        i = base + 2 * k
        pair = jnp.concatenate([patch_ref[i], patch_ref[i + 1]], axis=1)
        z = jnp.dot(weight, pair, preferred_element_type=F32)
        z_ref[i] = z[:, :WIDE]
        z_ref[i + 1] = z[:, WIDE:]


def pipelined(first, last, rows, make, use):
    make(first)

    def body(step, carry):
        base = first + rows * step
        use(base - rows)
        make(base)
        return carry

    lax.fori_loop(1, (last - first) // rows, body, 0)
    use(last - rows)


def main_kernel(
    place_ref,
    mixed_ref,
    part0_ref,
    part1_ref,
    part2_ref,
    part3_ref,
    forward_ref,
    backward_ref,
    w_out_ref,
    direct_ref,
    terms_ref,
    grad_ref,
    last_ref,
    round_ref,
    slope0_ref,
    state_ref,
    slope1_ref,
    slope2_ref,
    za_ref,
    zb_ref,
    patch0_ref,
    patch1_ref,
    patch2_ref,
    masked_ref,
    patchb_ref,
    upstream_ref,
    grad2_ref,
):
    row = place_ref[0]
    col = place_ref[1]
    rates = [place_ref[2], place_ref[3], place_ref[4]]
    inside = lane_mask(col)
    patch_refs = (patch0_ref, patch1_ref, patch2_ref)
    parts = (part0_ref, part1_ref, part2_ref, part3_ref)
    w_out = w_out_ref[...]
    z_refs = (za_ref, zb_ref)

    for n in range(4):

        def start(q, carry, n=n):
            given = parts[n][q].astype(F32)
            state_ref[HALO * n + q] = (mixed_ref[HALO * n + q] + given).astype(BF16)
            return carry

        lax.fori_loop(0, HALO, start, 0, unroll=4)

    for layer in range(3):
        z_now = z_refs[layer % 2]
        z_last = z_refs[(layer + 1) % 2]
        slope_ref = (slope0_ref, slope1_ref, slope2_ref)[layer]

        def make(base, layer=layer, z_last=z_last, slope_ref=slope_ref):
            block = pl.ds(base, ROWS)
            state = state_ref[block].astype(F32)
            if layer > 0:
                new = (state + many_taps(z_last, base, ROWS, rates[layer - 1])).astype(BF16)
                state_ref[block] = new
                state = new.astype(F32)
            act, slope = gelu_pair(state)
            slope_ref[block] = slope
            act = act * rows_mask(inside, row, base, ROWS)
            patch_refs[layer][block] = shifted_rows(act, rates[layer])

        def use(base, layer=layer, z_now=z_now):
            multiply(forward_ref[layer], patch_refs[layer], z_now, base, ROWS)

        pipelined(8 * layer, WIDE - 8 * layer, ROWS, make, use)

    def finish(step, carry):
        base = HALO + ROWS * step
        new = state_ref[pl.ds(base, ROWS)].astype(F32) + many_taps(za_ref, base, ROWS, rates[2])
        new = new.astype(BF16).astype(F32)
        direct_ref[pl.ds(base - HALO, ROWS), :] = jnp.sum(new * w_out[None], axis=1)[:, :TILE]
        return carry

    lax.fori_loop(0, TILE // ROWS, finish, 0)

    for n in range(4):
        upstream_ref[HALO * n : HALO * n + HALO, :] = parts[n][32].astype(F32) + parts[n][33].astype(F32)

    tile_lanes = jnp.where(lax.broadcasted_iota(jnp.int32, (1, WIDE), 1) < TILE, 1.0, 0.0).astype(F32)
    masked_ref[...] = jnp.zeros_like(masked_ref)

    def weight_terms(layer):
        def keep(step, carry):
            block = pl.ds(HALO + 8 * step, 8)
            masked_ref[block] = (round_ref[block].astype(F32) * tile_lanes[None]).astype(BF16)
            return carry

        lax.fori_loop(0, TILE // 8, keep, 0)
        rate = rates[layer]

        def body(step, total):
            base = 24 + 8 * step
            for part in range(2):
                at = base + 4 * part
                left = jnp.concatenate(
                    [
                        jnp.concatenate([masked_ref[at + k + off] for k in range(4)], axis=1)
                        for off in (rate, 0, -rate)
                    ],
                    axis=0,
                )
                right = jnp.concatenate([patch_refs[layer][at + k] for k in range(4)], axis=1)
                total = total + lax.dot_general(
                    left, right, (((1,), (1,)), ((), ())), preferred_element_type=F32
                )
            return total

        return lax.fori_loop(0, 10, body, jnp.zeros((96, 96), F32))

    def back(layer, first, last, one_grad, z_now):
        def make(base):
            rounded = one_grad(base).astype(BF16)
            round_ref[pl.ds(base, ROWS)] = rounded
            patchb_ref[pl.ds(base, ROWS)] = shifted_rows(rounded.astype(F32), rates[layer])

        def use(base):
            multiply(backward_ref[layer], patchb_ref, z_now, base, ROWS)

        pipelined(first, last, ROWS, make, use)
        return weight_terms(layer)

    def first_grad(base):
        return upstream_ref[pl.ds(base, ROWS), :][:, None, :] * w_out[None]

    def second_grad(base):
        block = pl.ds(base, ROWS)
        new = first_grad(base) + many_taps(zb_ref, base, ROWS, rates[2]) * slope2_ref[block]
        new = new * rows_mask(inside, row, base, ROWS)
        grad2_ref[block] = new
        return new

    terms2 = back(2, 8, 120, first_grad, zb_ref)
    terms1 = back(1, 16, 112, second_grad, za_ref)

    def third_grad(step, carry):
        base = 24 + ROWS * step
        block = pl.ds(base, ROWS)
        new = grad2_ref[block] + many_taps(za_ref, base, ROWS, rates[1]) * slope1_ref[block]
        new = new * rows_mask(inside, row, base, ROWS)
        rounded = new.astype(BF16)
        last_ref[pl.ds(base - 24, ROWS)] = rounded
        round_ref[block] = rounded
        slope = pltpu.roll(slope0_ref[block], TILE, 2)
        grad_ref[pl.ds(base - 24, ROWS)] = jnp.where(first_half, new, slope)
        return carry

    first_half = lax.broadcasted_iota(jnp.int32, (1, 1, WIDE), 2) < TILE
    lax.fori_loop(0, 80 // ROWS, third_grad, 0)
    terms0 = weight_terms(0)
    terms = jnp.concatenate([terms0, terms1, terms2], axis=0)
    spare = jnp.concatenate([terms[216:288, 32 * k : 32 * k + 32] for k in range(3)], axis=0)
    terms_ref[...] = jnp.concatenate([terms[0:216], spare], axis=1).astype(BF16)


def last_kernel(
    place_ref,
    grad_ref,
    round_ref,
    rows_ref,
    cols_ref,
    backward_ref,
    w_in_ref,
    row_ref,
    col_ref,
    z_ref,
    patch_ref,
):
    rate = place_ref[2]

    def make(base):
        patch_ref[pl.ds(base, ROWS)] = shifted_rows(round_ref[pl.ds(base, ROWS)].astype(F32), rate)

    def use(base):
        multiply(backward_ref[0], patch_ref, z_ref, base, ROWS)

    pipelined(0, 80, ROWS, make, use)
    w_in = w_in_ref[...]
    cols = cols_ref[0:TILE, :]

    def body(step, total):
        base = ROWS * step
        both = grad_ref[pl.ds(base + 8, ROWS)]
        slope = pltpu.roll(both, TILE, 2)
        start = both + many_taps(z_ref, base + 8, ROWS, rate) * slope
        start = start[:, :, :TILE].astype(BF16)
        rows = rows_ref[pl.ds(base + HALO, ROWS), :]
        sums = []
        for k in range(ROWS):
            hidden = lax.dot_general(
                start[k], w_in, (((0,), (0,)), ((), ())), preferred_element_type=F32
            )
            outer = hidden * gelu_pair(rows[k : k + 1, :] + cols)[1]
            sums.append(jnp.sum(outer, axis=0, keepdims=True))
            total = total + outer
        row_ref[pl.ds(base, ROWS), :] = jnp.concatenate(sums, axis=0).astype(BF16)
        return total

    total = lax.fori_loop(0, TILE // ROWS, body, jnp.zeros((TILE, 128), F32))
    col_ref[...] = total.astype(BF16)


def finish_kernel(
    mine_ref,
    got_ref,
    col_ref,
    w_left_ref,
    w_right_ref,
    direct_ref,
    other_ref,
    logits_ref,
    grad_rows_ref,
    grad_cols_ref,
    conv_ref,
):
    logits_ref[...] = 0.5 * (direct_ref[...] + other_ref[...].T)
    total = mine_ref[...].astype(F32) + got_ref[...].astype(F32)
    for value, weight_ref, out_ref in (
        (total[0:TILE], w_left_ref, grad_rows_ref),
        (col_ref[...].astype(F32), w_right_ref, grad_cols_ref),
    ):
        out_ref[...] = lax.dot_general(
            value,
            weight_ref[...].astype(F32),
            (((1,), (1,)), ((), ())),
            precision=lax.Precision.HIGHEST,
            preferred_element_type=F32,
        )
    terms = total[TILE:] * (1.0 / 1024.0)
    spare = jnp.concatenate([terms[72 * k : 72 * k + 72, 96:128] for k in range(3)], axis=1)
    terms = jnp.concatenate([terms[:, 0:96], spare], axis=0)
    for layer in range(3):
        at = 96 * layer
        conv_ref[layer] = jnp.concatenate(
            [terms[at + CH * a : at + CH * a + CH] for a in range(3)], axis=1
        )


def shape(*dims, dtype=F32):
    return jax.ShapeDtypeStruct(dims, dtype)


def call(kernel, outs, specs, scratch=(), mib=8, cost=1):
    return pl.pallas_call(
        kernel,
        out_shape=outs,
        in_specs=specs,
        out_specs=[VMEM] * len(outs),
        scratch_shapes=list(scratch),
        compiler_params=pltpu.CompilerParams(vmem_limit_bytes=mib * 2**20),
        cost_estimate=pl.CostEstimate(
            flops=cost * 10**9, bytes_accessed=cost * 3 * 10**6, transcendentals=0
        ),
    )


def on_device(features, w_left, w_right, w_in, pair_input, conv_w, w_out, dilation, cotangent):
    n_row = lax.axis_size("row")
    n_col = lax.axis_size("col")
    row_at = lax.axis_index("row").astype(jnp.int32)
    col_at = lax.axis_index("col").astype(jnp.int32)
    place = jnp.concatenate([jnp.stack([row_at, col_at]), dilation, jnp.zeros((3,), jnp.int32)])
    up = [(i, i + 1) for i in range(n_row - 1)]
    down = [(i + 1, i) for i in range(n_row - 1)]
    swap = [(r * n_col + c, c * n_col + r) for r in range(n_row) for c in range(n_col)]

    mirrored = lax.ppermute(cotangent, ("row", "col"), swap)
    (sent,) = call(
        spread_kernel, [shape(n_row * n_col, *features.shape, dtype=BF16)], [VMEM]
    )(features)
    gathered = lax.all_to_all(sent, ("row", "col"), 0, 0)
    own, left_edge, right_edge, upstream = call(
        edges_kernel,
        [shape(TILE, CH, TILE, dtype=BF16)]
        + [shape(17, CH, WIDE, dtype=BF16)] * 2
        + [shape(TILE, TILE)],
        [VMEM] * 3,
        (),
        8,
        12,
    )(pair_input, cotangent, mirrored)
    from_left = lax.ppermute(right_edge, "col", up)
    from_right = lax.ppermute(left_edge, "col", down)

    mixed, row_project, col_project, forward_w, backward_w = call(
        mixed_kernel,
        [shape(WIDE, CH, WIDE), shape(WIDE, 128), shape(WIDE, 128)]
        + [shape(3, 96, 96, dtype=BF16)] * 2,
        [SMEM] + [VMEM] * 5,
        [pltpu.VMEM((WIDE, 128), F32)],
        16,
        6,
    )(place, gathered, w_left, w_right, w_in, conv_w)
    from_left, from_right, mixed = lax.optimization_barrier((from_left, from_right, mixed))

    upper, lower = call(
        widen_kernel, [shape(HALO + 2, CH, WIDE, dtype=BF16)] * 2, [VMEM] * 4
    )(own, upstream, from_left, from_right)
    above = lax.ppermute(lower, "row", up)
    below = lax.ppermute(upper, "row", down)

    w_out_wide = jnp.broadcast_to(w_out.astype(F32)[:, None], (CH, WIDE))
    big = (WIDE, CH, WIDE)
    direct, terms, grad, rounded = call(
        main_kernel,
        [shape(TILE, TILE), shape(216, 128, dtype=BF16), shape(80, CH, WIDE), shape(80, CH, WIDE, dtype=BF16)],
        [SMEM] + [VMEM] * 8,
        [
            pltpu.VMEM(big, BF16),
            pltpu.VMEM(big, F32),
            pltpu.VMEM(big, BF16),
            pltpu.VMEM(big, F32),
            pltpu.VMEM(big, F32),
            pltpu.VMEM((WIDE, 96, WIDE), F32),
            pltpu.VMEM((WIDE, 96, WIDE), F32),
            pltpu.VMEM((WIDE, 96, WIDE), BF16),
            pltpu.VMEM((WIDE, 96, WIDE), BF16),
            pltpu.VMEM((WIDE, 96, WIDE), BF16),
            pltpu.VMEM(big, BF16),
            pltpu.VMEM((WIDE, 96, WIDE), BF16),
            pltpu.VMEM((WIDE, WIDE), F32),
            pltpu.VMEM(big, F32),
        ],
        42,
        24,
    )(place, mixed, above, upper, lower, below, forward_w, backward_w, w_out_wide)

    def flipped(value, row_bits, col_bits):
        pairs = [
            (r * n_col + c, (r ^ row_bits) * n_col + (c ^ col_bits))
            for r in range(n_row)
            for c in range(n_col)
        ]
        return lax.ppermute(value, ("row", "col"), pairs)

    def summed(value, row_bits, col_bits):
        return (value.astype(F32) + flipped(value, row_bits, col_bits).astype(F32)).astype(BF16)

    direct_other = lax.ppermute(direct, ("row", "col"), swap)
    terms = summed(terms, 1, 0)
    grad, rounded, row_project, col_project, terms = lax.optimization_barrier(
        (grad, rounded, row_project, col_project, terms)
    )
    terms = summed(terms, 2, 0)
    row_part, col_part = call(
        last_kernel,
        [shape(TILE, 128, dtype=BF16), shape(TILE, 128, dtype=BF16)],
        [SMEM] + [VMEM] * 6,
        [pltpu.VMEM((80, 96, WIDE), F32), pltpu.VMEM((80, 96, WIDE), BF16)],
        16,
        7,
    )(place, grad, rounded, row_project, col_project, backward_w, w_in)

    packed = jnp.concatenate([col_part, terms], axis=0)
    packed = summed(packed, 4, 0)
    row_part = summed(row_part, 0, 1)
    packed = summed(packed, 12, 0)
    col_part = packed[:TILE]
    terms = summed(packed[TILE:], 2, 1)
    col_part = summed(col_part, 1, 0)
    packed = jnp.concatenate([row_part, terms], axis=0)
    packed = summed(packed, 0, 2)
    col_part = summed(col_part, 2, 0)
    packed = summed(packed, 0, 4)
    return tuple(
        call(
            finish_kernel,
            [shape(TILE, TILE), shape(TILE, 128), shape(TILE, 128), shape(3, CH, 288)],
            [VMEM] * 7,
        )(packed, flipped(packed, 0, 12), col_part, w_left, w_right, direct, direct_other)
    )


def solution(mesh):
    return jax.shard_map(
        on_device,
        mesh=mesh,
        in_specs=(
            P(("row", "col"), None),
            P(),
            P(),
            P(),
            P(None, "row", "col"),
            P(),
            P(),
            P(),
            P("row", "col"),
        ),
        out_specs=(P("row", "col"), P("row", None), P("col", None), P()),
        check_vma=False,
    )
```

```python
import jax
import jax.numpy as jnp
from jax import lax
from jax.experimental import pallas as pl
from jax.experimental.pallas import tpu as pltpu
from jax.sharding import PartitionSpec as P

F32 = jnp.float32
BF16 = jnp.bfloat16
K_ROOT = 0.7978845608028654
CUBIC = 0.044715
TILE = 64
HALO = 32
WIDE = TILE + 2 * HALO
CH = 32
ROWS = 16
VMEM = pl.BlockSpec(memory_space=pltpu.VMEM)
SMEM = pl.BlockSpec(memory_space=pltpu.SMEM)


def gelu(value):
    inner = value * (K_ROOT + (K_ROOT * CUBIC) * (value * value))
    half = 0.5 * value
    return half + half * jnp.tanh(inner)


def gelu_pair(value):
    square = value * value
    tangent = jnp.tanh(value * (K_ROOT + (K_ROOT * CUBIC) * square))
    half = 0.5 * value
    up = 0.5 + 0.5 * tangent
    result = value * up
    slope = up + half * (1.0 - tangent * tangent) * (K_ROOT + (3.0 * K_ROOT * CUBIC) * square)
    return result, slope


def split(value):
    high = value.astype(BF16)
    return high, (value - high.astype(F32)).astype(BF16)


def spread_kernel(feat_ref, sent_ref):
    sent_ref[...] = jnp.broadcast_to(feat_ref[...][None], sent_ref.shape)


def edges_kernel(
    pair_ref, cot_ref, mirror_ref, own_ref, left_ref, right_ref, upstream_ref
):
    own = jnp.swapaxes(pair_ref[...].astype(F32), 0, 1)
    own_ref[...] = own.astype(BF16)
    cot = 0.5 * (cot_ref[...] + mirror_ref[...].T)
    upstream_ref[...] = cot
    for out_ref, first in ((left_ref, 0), (right_ref, TILE - HALO)):
        last = first + HALO
        for q in range(16):
            out_ref[q] = jnp.concatenate(
                [own[q + 16 * m, :, first:last] for m in range(4)], axis=1
            ).astype(BF16)
        edge = jnp.concatenate([cot[16 * m : 16 * m + 16, first:last] for m in range(4)], axis=1)
        high, low = split(edge)
        out_ref[16, 0:16, :] = high
        out_ref[16, 16:32, :] = low


def widen_kernel(own_ref, upstream_ref, from_left_ref, from_right_ref, upper_ref, lower_ref):
    cot = upstream_ref[...]
    for m in range(4):
        out_ref = (upper_ref, lower_ref)[m // 2]
        lanes = slice(HALO * m, HALO * m + HALO)
        base = 16 * (m % 2)
        for q in range(16):
            out_ref[base + q] = jnp.concatenate(
                [
                    own_ref[16 * m + q].astype(F32),
                    from_right_ref[q].astype(F32)[:, lanes],
                    from_left_ref[q].astype(F32)[:, lanes],
                ],
                axis=1,
            ).astype(BF16)
        high, low = split(cot[16 * m : 16 * m + 16, :])
        for part, row, at in ((high, 32, 0), (low, 33, 16)):
            out_ref[row, base : base + 16, :] = jnp.concatenate(
                [
                    part.astype(F32),
                    from_right_ref[16, at : at + 16, :].astype(F32)[:, lanes],
                    from_left_ref[16, at : at + 16, :].astype(F32)[:, lanes],
                ],
                axis=1,
            ).astype(BF16)


def mixed_kernel(
    place_ref, feat_ref, w_left_ref, w_right_ref, w_in_ref, conv_ref,
    mixed_ref, rows_ref, cols_ref, backward_ref, picked_ref,
):
    row = place_ref[0]
    col = place_ref[1]
    row_chunks = [jnp.maximum(2 * row - 1, 0), 2 * row, 2 * row + 1, jnp.minimum(2 * row + 2, 31)]
    col_chunks = [2 * col, 2 * col + 1, jnp.minimum(2 * col + 2, 31), jnp.maximum(2 * col - 1, 0)]
    for chunks, weight_ref, out_ref in (
        (row_chunks, w_left_ref, rows_ref),
        (col_chunks, w_right_ref, cols_ref),
    ):
        for n, chunk in enumerate(chunks):
            for m in range(8):
                at = HALO * n + 4 * m
                picked_ref[at : at + 4, :] = feat_ref[8 * chunk + m].astype(F32)
        out_ref[...] = jnp.dot(
            picked_ref[...].astype(BF16), weight_ref[...], preferred_element_type=F32
        )
    for layer in range(3):
        turned = jnp.concatenate([conv_ref[layer].astype(F32), jnp.zeros((CH, 96), F32)], axis=1)
        turned = jnp.concatenate([turned[:, 128 * k : 128 * k + 128].T for k in range(3)], axis=0)
        backward_ref[layer] = jnp.concatenate(
            [turned[CH * tap : CH * tap + CH] for tap in range(8, -1, -1)], axis=1
        ).astype(BF16)
    w_in = w_in_ref[...]

    def body(step, carry):
        cols = cols_ref[...]
        rows = rows_ref[pl.ds(ROWS * step, ROWS), :]
        for k in range(0, ROWS, 2):
            pair = [gelu(rows[k + i : k + i + 1, :] + cols).astype(BF16) for i in range(2)]
            out = lax.dot_general(
                w_in, jnp.concatenate(pair, 0), (((1,), (1,)), ((), ())), preferred_element_type=F32
            )
            for i in range(2):
                mixed_ref[ROWS * step + k + i] = out[:, WIDE * i : WIDE * i + WIDE]
        return carry

    lax.fori_loop(0, WIDE // ROWS, body, 0)


def lane_mask(col):
    lane = lax.broadcasted_iota(jnp.int32, (1, WIDE), 1)
    bin_at = TILE * col + jnp.where(lane < TILE + HALO, lane, lane - WIDE)
    return jnp.where((bin_at >= 0) & (bin_at < 1024), 1.0, 0.0).astype(F32)


def shifted_rows(value, rate):
    return jnp.concatenate(
        [pltpu.roll(value, rate, 2), value, pltpu.roll(value, WIDE - rate, 2)], axis=1
    ).astype(BF16)


def rows_mask(inside, row, base, rows):
    at = TILE * row - HALO + base + lax.broadcasted_iota(jnp.int32, (rows, 1, 1), 0)
    return jnp.where((at >= 0) & (at < 1024), 1.0, 0.0).astype(F32) * inside[None]


def convolve(weight, patch_ref, out_ref, base, rows, rate):
    for k in range(rows // 2):
        i = base + 2 * k
        taps = [
            jnp.concatenate([patch_ref[i + off], patch_ref[i + off + 1]], axis=1)
            for off in (-rate, 0, rate)
        ]
        z = jnp.dot(weight, jnp.concatenate(taps, axis=0), preferred_element_type=F32)
        out_ref[i] = z[:, :WIDE]
        out_ref[i + 1] = z[:, WIDE:]


def pipelined(first, last, rows, make, use, beside=None):
    make(first)

    def body(step, carry):
        base = first + rows * step
        use(base - rows)
        make(base)
        if beside is not None:
            beside(step - 1)
        return carry

    blocks = (last - first) // rows
    lax.fori_loop(1, blocks, body, 0)
    use(last - rows)
    return blocks - 1


def main_kernel(
    place_ref,
    mixed_ref,
    part0_ref,
    part1_ref,
    part2_ref,
    part3_ref,
    forward_ref,
    backward_ref,
    w_out_ref,
    direct_ref,
    terms_ref,
    grad_ref,
    last_ref,
    slope0_ref,
    slope1_ref,
    slope2_ref,
    state_ref,
    z_ref,
    patch0_ref,
    patch1_ref,
    patch2_ref,
    patch3_ref,
    patch4_ref,
    masked0_ref,
    masked1_ref,
    upstream_ref,
    grad2_ref,
    total_ref,
):
    row = place_ref[0]
    col = place_ref[1]
    rates = [place_ref[2], place_ref[3], place_ref[4]]
    inside = lane_mask(col)
    patch_refs = (patch0_ref, patch1_ref, patch2_ref)
    slope_refs = (slope0_ref, slope1_ref, slope2_ref)
    parts = (part0_ref, part1_ref, part2_ref, part3_ref)
    w_out = w_out_ref[...]

    def activate(layer, base, state):
        block = pl.ds(base, ROWS)
        state_ref[block] = state
        act, slope = gelu_pair(state.astype(F32))
        slope_refs[layer][block] = slope.astype(BF16)
        act = act * rows_mask(inside, row, base, ROWS)
        patch_refs[layer][block] = shifted_rows(act, rates[layer])

    for n in range(4):

        def start(step, carry, n=n):
            at = ROWS * step
            given = parts[n][pl.ds(at, ROWS)].astype(F32)
            base = HALO * n + at
            activate(0, base, (mixed_ref[pl.ds(base, ROWS)] + given).astype(BF16))
            return carry

        lax.fori_loop(0, HALO // ROWS, start, 0)

    def next_state(base):
        block = pl.ds(base, ROWS)
        return (state_ref[block].astype(F32) + z_ref[block]).astype(BF16)

    for layer in (1, 2):

        def make(base, layer=layer):
            convolve(
                forward_ref[layer - 1], patch_refs[layer - 1], z_ref, base, ROWS, rates[layer - 1]
            )

        def use(base, layer=layer):
            activate(layer, base, next_state(base))

        pipelined(8 * layer, WIDE - 8 * layer, ROWS, make, use)

    for n in range(4):
        upstream_ref[HALO * n : HALO * n + HALO, :] = parts[n][32].astype(F32) + parts[n][33].astype(F32)
    tile_lanes = jnp.where(lax.broadcasted_iota(jnp.int32, (1, WIDE), 1) < TILE, 1.0, 0.0).astype(F32)

    def keep(ref, base, rounded):
        at = base + lax.broadcasted_iota(jnp.int32, (ROWS, 1, 1), 0)
        own = jnp.where((at >= HALO) & (at < HALO + TILE), 1.0, 0.0).astype(F32) * tile_lanes[None]
        ref[pl.ds(base, ROWS)] = (rounded.astype(F32) * own).astype(BF16)

    def first_grad(base):
        return upstream_ref[pl.ds(base, ROWS), :][:, None, :] * w_out[None]

    def last_make(base):
        convolve(forward_ref[2], patch2_ref, z_ref, base, ROWS, rates[2])

    def last_use(base):
        new = next_state(base).astype(F32)
        direct_ref[pl.ds(base - HALO, ROWS), :] = jnp.sum(new * w_out[None], axis=1)[:, :TILE]

    def begin(step):
        base = 8 + ROWS * step
        rounded = first_grad(base).astype(BF16)
        keep(masked0_ref, base, rounded)
        patch3_ref[pl.ds(base, ROWS)] = shifted_rows(rounded.astype(F32), rates[2])

    pipelined(HALO, HALO + TILE, ROWS, last_make, last_use, begin)
    for step in (3, 4, 5, 6):
        begin(step)

    total_ref[...] = jnp.zeros_like(total_ref)

    def weight_terms(layer, masked_ref, step):
        rate = rates[layer]
        total = total_ref[layer]
        for part in range(4):
            at = 24 + ROWS * step + 4 * part
            left = jnp.concatenate(
                [
                    jnp.concatenate([masked_ref[at + k + off] for k in range(4)], axis=1)
                    for off in (rate, 0, -rate)
                ],
                axis=0,
            )
            right = jnp.concatenate([patch_refs[layer][at + k] for k in range(4)], axis=1)
            total = total + lax.dot_general(
                left, right, (((1,), (1,)), ((), ())), preferred_element_type=F32
            )
        total_ref[layer] = total

    def second_make(base):
        convolve(backward_ref[2], patch3_ref, z_ref, base, ROWS, rates[2])

    def second_use(base):
        block = pl.ds(base, ROWS)
        new = first_grad(base) + z_ref[block] * slope2_ref[block].astype(F32)
        new = new * rows_mask(inside, row, base, ROWS)
        grad2_ref[block] = new
        rounded = new.astype(BF16)
        keep(masked1_ref, base, rounded)
        patch4_ref[block] = shifted_rows(rounded.astype(F32), rates[1])

    pipelined(16, 112, ROWS, second_make, second_use, lambda step: weight_terms(2, masked0_ref, step))

    first_half = lax.broadcasted_iota(jnp.int32, (1, 1, WIDE), 2) < TILE

    def third_make(base):
        convolve(backward_ref[1], patch4_ref, z_ref, base, ROWS, rates[1])

    def third_use(base):
        block = pl.ds(base, ROWS)
        new = grad2_ref[block] + z_ref[block] * slope1_ref[block].astype(F32)
        new = new * rows_mask(inside, row, base, ROWS)
        rounded = new.astype(BF16)
        keep(masked0_ref, base, rounded)
        last_ref[pl.ds(base - 24, ROWS)] = rounded
        slope = pltpu.roll(slope0_ref[block].astype(F32), TILE, 2)
        grad_ref[pl.ds(base - 24, ROWS)] = jnp.where(first_half, new, slope)

    done = pipelined(24, 104, ROWS, third_make, third_use, lambda step: weight_terms(1, masked1_ref, step))
    weight_terms(1, masked1_ref, done)
    for step in range(5):
        weight_terms(0, masked0_ref, step)
    terms = jnp.concatenate([total_ref[layer] for layer in range(3)], axis=0)
    spare = jnp.concatenate([terms[216:288, 32 * k : 32 * k + 32] for k in range(3)], axis=0)
    terms_ref[...] = jnp.concatenate([terms[0:216], spare], axis=1).astype(BF16)


def last_kernel(
    place_ref,
    grad_ref,
    round_ref,
    rows_ref,
    cols_ref,
    backward_ref,
    w_in_ref,
    row_ref,
    col_ref,
    z_ref,
    patch_ref,
    total_ref,
):
    rate = place_ref[2]

    def spread(step, carry):
        block = pl.ds(ROWS * step, ROWS)
        patch_ref[block] = shifted_rows(round_ref[block].astype(F32), rate)
        return carry

    lax.fori_loop(0, 80 // ROWS, spread, 0)
    w_in = w_in_ref[...]
    cols = cols_ref[0:TILE, :]

    def make(base):
        convolve(backward_ref[0], patch_ref, z_ref, base, ROWS, rate)

    def use(base):
        block = pl.ds(base, ROWS)
        both = grad_ref[block]
        slope = pltpu.roll(both, TILE, 2)
        start = (both + z_ref[block] * slope)[:, :, :TILE].astype(BF16)
        rows = rows_ref[pl.ds(base + 24, ROWS), :]
        sums = []
        total = total_ref[...]
        for k in range(ROWS):
            hidden = lax.dot_general(
                start[k], w_in, (((0,), (0,)), ((), ())), preferred_element_type=F32
            )
            outer = hidden * gelu_pair(rows[k : k + 1, :] + cols)[1]
            sums.append(jnp.sum(outer, axis=0, keepdims=True))
            total = total + outer
        total_ref[...] = total
        row_ref[pl.ds(base - 8, ROWS), :] = jnp.concatenate(sums, axis=0).astype(BF16)

    total_ref[...] = jnp.zeros_like(total_ref)
    pipelined(8, 8 + TILE, ROWS, make, use)
    col_ref[...] = total_ref[...].astype(BF16)


def finish_kernel(
    mine_ref,
    got_ref,
    col_ref,
    w_left_ref,
    w_right_ref,
    direct_ref,
    other_ref,
    logits_ref,
    grad_rows_ref,
    grad_cols_ref,
    conv_ref,
):
    logits_ref[...] = 0.5 * (direct_ref[...] + other_ref[...].T)
    total = mine_ref[...].astype(F32) + got_ref[...].astype(F32)
    for value, weight_ref, out_ref in (
        (total[0:TILE], w_left_ref, grad_rows_ref),
        (col_ref[...].astype(F32), w_right_ref, grad_cols_ref),
    ):
        out_ref[...] = lax.dot_general(
            value,
            weight_ref[...].astype(F32),
            (((1,), (1,)), ((), ())),
            precision=lax.Precision.HIGHEST,
            preferred_element_type=F32,
        )
    terms = total[TILE:] * (1.0 / 1024.0)
    spare = jnp.concatenate([terms[72 * k : 72 * k + 72, 96:128] for k in range(3)], axis=1)
    terms = jnp.concatenate([terms[:, 0:96], spare], axis=0)
    for layer in range(3):
        at = 96 * layer
        conv_ref[layer] = jnp.concatenate(
            [terms[at + CH * a : at + CH * a + CH] for a in range(3)], axis=1
        )


def shape(*dims, dtype=F32):
    return jax.ShapeDtypeStruct(dims, dtype)


def call(kernel, outs, specs, scratch=(), mib=8, cost=1):
    return pl.pallas_call(
        kernel,
        out_shape=outs,
        in_specs=specs,
        out_specs=[VMEM] * len(outs),
        scratch_shapes=list(scratch),
        compiler_params=pltpu.CompilerParams(vmem_limit_bytes=mib * 2**20),
        cost_estimate=pl.CostEstimate(
            flops=cost * 10**9, bytes_accessed=cost * 3 * 10**6, transcendentals=0
        ),
    )


def on_device(features, w_left, w_right, w_in, pair_input, conv_w, w_out, dilation, cotangent):
    n_row = lax.axis_size("row")
    n_col = lax.axis_size("col")
    row_at = lax.axis_index("row").astype(jnp.int32)
    col_at = lax.axis_index("col").astype(jnp.int32)
    place = jnp.concatenate([jnp.stack([row_at, col_at]), dilation, jnp.zeros((3,), jnp.int32)])
    up = [(i, i + 1) for i in range(n_row - 1)]
    down = [(i + 1, i) for i in range(n_row - 1)]
    swap = [(r * n_col + c, c * n_col + r) for r in range(n_row) for c in range(n_col)]

    mirrored = lax.ppermute(cotangent, ("row", "col"), swap)
    (sent,) = call(
        spread_kernel, [shape(n_row * n_col, *features.shape, dtype=BF16)], [VMEM]
    )(features)
    gathered = lax.all_to_all(sent, ("row", "col"), 0, 0)
    own, left_edge, right_edge, upstream = call(
        edges_kernel,
        [shape(TILE, CH, TILE, dtype=BF16)]
        + [shape(17, CH, WIDE, dtype=BF16)] * 2
        + [shape(TILE, TILE)],
        [VMEM] * 3,
        (),
        8,
        12,
    )(pair_input, cotangent, mirrored)
    from_left = lax.ppermute(right_edge, "col", up)
    from_right = lax.ppermute(left_edge, "col", down)

    upper, lower = call(
        widen_kernel, [shape(HALO + 2, CH, WIDE, dtype=BF16)] * 2, [VMEM] * 4
    )(own, upstream, from_left, from_right)
    above = lax.ppermute(lower, "row", up)
    below = lax.ppermute(upper, "row", down)

    mixed, row_project, col_project, backward_w = call(
        mixed_kernel,
        [shape(WIDE, CH, WIDE), shape(WIDE, 128), shape(WIDE, 128)]
        + [shape(3, CH, 288, dtype=BF16)],
        [SMEM] + [VMEM] * 5,
        [pltpu.VMEM((WIDE, 128), F32)],
        16,
        6,
    )(place, gathered, w_left, w_right, w_in, conv_w)
    w_out_wide = jnp.broadcast_to(w_out.astype(F32)[:, None], (CH, WIDE))
    big = (WIDE, CH, WIDE)
    direct, terms, grad, rounded = call(
        main_kernel,
        [shape(TILE, TILE), shape(216, 128, dtype=BF16), shape(80, CH, WIDE), shape(80, CH, WIDE, dtype=BF16)],
        [SMEM] + [VMEM] * 8,
        [pltpu.VMEM(big, BF16)] * 4
        + [pltpu.VMEM(big, F32)]
        + [pltpu.VMEM((WIDE, 96, WIDE), BF16)] * 5
        + [pltpu.VMEM(big, BF16)] * 2
        + [pltpu.VMEM((WIDE, WIDE), F32), pltpu.VMEM(big, F32), pltpu.VMEM((3, 96, 96), F32)],
        36,
        24,
    )(place, mixed, above, upper, lower, below, conv_w, backward_w, w_out_wide)

    def flipped(value, row_bits, col_bits):
        pairs = [
            (r * n_col + c, (r ^ row_bits) * n_col + (c ^ col_bits))
            for r in range(n_row)
            for c in range(n_col)
        ]
        return lax.ppermute(value, ("row", "col"), pairs)

    def summed(value, row_bits, col_bits):
        return (value.astype(F32) + flipped(value, row_bits, col_bits).astype(F32)).astype(BF16)

    direct_other = lax.ppermute(direct, ("row", "col"), swap)
    terms = summed(terms, 1, 0)
    grad, rounded, row_project, col_project, terms = lax.optimization_barrier(
        (grad, rounded, row_project, col_project, terms)
    )
    terms = summed(terms, 2, 0)
    row_part, col_part = call(
        last_kernel,
        [shape(TILE, 128, dtype=BF16), shape(TILE, 128, dtype=BF16)],
        [SMEM] + [VMEM] * 6,
        [
            pltpu.VMEM((80, CH, WIDE), F32),
            pltpu.VMEM((80, 96, WIDE), BF16),
            pltpu.VMEM((TILE, 128), F32),
        ],
        16,
        7,
    )(place, grad, rounded, row_project, col_project, backward_w, w_in)

    packed = jnp.concatenate([col_part, terms], axis=0)
    packed = summed(packed, 4, 0)
    row_part = summed(row_part, 0, 1)
    packed = summed(packed, 12, 0)
    col_part = packed[:TILE]
    terms = summed(packed[TILE:], 2, 1)
    col_part = summed(col_part, 1, 0)
    packed = jnp.concatenate([row_part, terms], axis=0)
    packed = summed(packed, 0, 2)
    col_part = summed(col_part, 2, 0)
    packed = summed(packed, 0, 4)
    return tuple(
        call(
            finish_kernel,
            [shape(TILE, TILE), shape(TILE, 128), shape(TILE, 128), shape(3, CH, 288)],
            [VMEM] * 7,
        )(packed, flipped(packed, 0, 12), col_part, w_left, w_right, direct, direct_other)
    )


def solution(mesh):
    return jax.shard_map(
        on_device,
        mesh=mesh,
        in_specs=(
            P(("row", "col"), None),
            P(),
            P(),
            P(),
            P(None, "row", "col"),
            P(),
            P(),
            P(),
            P("row", "col"),
        ),
        out_specs=(P("row", "col"), P("row", None), P("col", None), P()),
        check_vma=False,
    )
```

```python
import jax
import jax.numpy as jnp
from jax import lax
from jax.experimental import pallas as pl
from jax.experimental.pallas import tpu as pltpu
from jax.sharding import PartitionSpec as P

F32 = jnp.float32
BF16 = jnp.bfloat16
K_ROOT = 0.7978845608028654
CUBIC = 0.044715
TILE = 64
HALO = 32
WIDE = TILE + 2 * HALO
CH = 32
ROWS = 16
VMEM = pl.BlockSpec(memory_space=pltpu.VMEM)
SMEM = pl.BlockSpec(memory_space=pltpu.SMEM)


def gelu(value):
    inner = value * (K_ROOT + (K_ROOT * CUBIC) * (value * value))
    half = 0.5 * value
    return half + half * jnp.tanh(inner)


def gelu_pair(value):
    square = value * value
    tangent = jnp.tanh(value * (K_ROOT + (K_ROOT * CUBIC) * square))
    half = 0.5 * value
    up = 0.5 + 0.5 * tangent
    result = value * up
    slope = up + half * (1.0 - tangent * tangent) * (K_ROOT + (3.0 * K_ROOT * CUBIC) * square)
    return result, slope


def split(value):
    high = value.astype(BF16)
    return high, (value - high.astype(F32)).astype(BF16)


def spread_kernel(feat_ref, sent_ref):
    sent_ref[...] = jnp.broadcast_to(feat_ref[...][None], sent_ref.shape)


def edges_kernel(
    pair_ref, cot_ref, mirror_ref, own_ref, left_ref, right_ref, upstream_ref
):
    own = jnp.swapaxes(pair_ref[...].astype(F32), 0, 1)
    own_ref[...] = own.astype(BF16)
    cot = 0.5 * (cot_ref[...] + mirror_ref[...].T)
    upstream_ref[...] = cot
    for out_ref, first in ((left_ref, 0), (right_ref, TILE - HALO)):
        last = first + HALO
        for q in range(16):
            out_ref[q] = jnp.concatenate(
                [own[q + 16 * m, :, first:last] for m in range(4)], axis=1
            ).astype(BF16)
        edge = jnp.concatenate([cot[16 * m : 16 * m + 16, first:last] for m in range(4)], axis=1)
        high, low = split(edge)
        out_ref[16, 0:16, :] = high
        out_ref[16, 16:32, :] = low


def widen_kernel(own_ref, upstream_ref, from_left_ref, from_right_ref, upper_ref, lower_ref):
    cot = upstream_ref[...]
    for m in range(4):
        out_ref = (upper_ref, lower_ref)[m // 2]
        lanes = slice(HALO * m, HALO * m + HALO)
        base = 16 * (m % 2)
        for q in range(16):
            out_ref[base + q] = jnp.concatenate(
                [
                    own_ref[16 * m + q].astype(F32),
                    from_right_ref[q].astype(F32)[:, lanes],
                    from_left_ref[q].astype(F32)[:, lanes],
                ],
                axis=1,
            ).astype(BF16)
        high, low = split(cot[16 * m : 16 * m + 16, :])
        for part, row, at in ((high, 32, 0), (low, 33, 16)):
            out_ref[row, base : base + 16, :] = jnp.concatenate(
                [
                    part.astype(F32),
                    from_right_ref[16, at : at + 16, :].astype(F32)[:, lanes],
                    from_left_ref[16, at : at + 16, :].astype(F32)[:, lanes],
                ],
                axis=1,
            ).astype(BF16)


def mixed_kernel(
    place_ref, feat_ref, w_left_ref, w_right_ref, w_in_ref, conv_ref,
    mixed_ref, rows_ref, cols_ref, backward_ref, picked_ref,
):
    row = place_ref[0]
    col = place_ref[1]
    row_chunks = [jnp.maximum(2 * row - 1, 0), 2 * row, 2 * row + 1, jnp.minimum(2 * row + 2, 31)]
    col_chunks = [2 * col, 2 * col + 1, jnp.minimum(2 * col + 2, 31), jnp.maximum(2 * col - 1, 0)]
    for chunks, weight_ref, out_ref in (
        (row_chunks, w_left_ref, rows_ref),
        (col_chunks, w_right_ref, cols_ref),
    ):
        for n, chunk in enumerate(chunks):
            for m in range(8):
                at = HALO * n + 4 * m
                picked_ref[at : at + 4, :] = feat_ref[8 * chunk + m].astype(F32)
        out_ref[...] = jnp.dot(
            picked_ref[...].astype(BF16), weight_ref[...], preferred_element_type=F32
        )
    for layer in range(3):
        turned = jnp.concatenate([conv_ref[layer].astype(F32), jnp.zeros((CH, 96), F32)], axis=1)
        turned = jnp.concatenate([turned[:, 128 * k : 128 * k + 128].T for k in range(3)], axis=0)
        backward_ref[layer] = jnp.concatenate(
            [turned[CH * tap : CH * tap + CH] for tap in range(8, -1, -1)], axis=1
        ).astype(BF16)
    w_in = w_in_ref[...]

    def body(step, carry):
        cols = cols_ref[...]
        rows = rows_ref[pl.ds(ROWS * step, ROWS), :]
        for k in range(0, ROWS, 2):
            pair = [gelu(rows[k + i : k + i + 1, :] + cols).astype(BF16) for i in range(2)]
            out = lax.dot_general(
                w_in, jnp.concatenate(pair, 0), (((1,), (1,)), ((), ())), preferred_element_type=F32
            )
            for i in range(2):
                mixed_ref[ROWS * step + k + i] = out[:, WIDE * i : WIDE * i + WIDE]
        return carry

    lax.fori_loop(0, WIDE // ROWS, body, 0)


def lane_mask(col):
    lane = lax.broadcasted_iota(jnp.int32, (1, WIDE), 1)
    bin_at = TILE * col + jnp.where(lane < TILE + HALO, lane, lane - WIDE)
    return jnp.where((bin_at >= 0) & (bin_at < 1024), 1.0, 0.0).astype(F32)


def shifted_rows(value, rate):
    return jnp.concatenate(
        [pltpu.roll(value, rate, 2), value, pltpu.roll(value, WIDE - rate, 2)], axis=1
    ).astype(BF16)


def rows_mask(inside, row, base, rows):
    at = TILE * row - HALO + base + lax.broadcasted_iota(jnp.int32, (rows, 1, 1), 0)
    return jnp.where((at >= 0) & (at < 1024), 1.0, 0.0).astype(F32) * inside[None]


def convolve(weight, patch_ref, out_ref, base, rows, rate):
    for k in range(rows // 2):
        i = base + 2 * k
        taps = [
            jnp.concatenate([patch_ref[i + off], patch_ref[i + off + 1]], axis=1)
            for off in (-rate, 0, rate)
        ]
        z = jnp.dot(weight, jnp.concatenate(taps, axis=0), preferred_element_type=F32)
        out_ref[i] = z[:, :WIDE]
        out_ref[i + 1] = z[:, WIDE:]


def pipelined(first, last, rows, make, use, beside=None):
    make(first)

    def body(step, carry):
        base = first + rows * step
        use(base - rows)
        make(base)
        if beside is not None:
            beside(step - 1)
        return carry

    blocks = (last - first) // rows
    for step in range(1, blocks):
        body(step, 0)
    use(last - rows)
    return blocks - 1


def main_kernel(
    place_ref,
    mixed_ref,
    part0_ref,
    part1_ref,
    part2_ref,
    part3_ref,
    forward_ref,
    backward_ref,
    w_out_ref,
    direct_ref,
    terms_ref,
    grad_ref,
    last_ref,
    slope0_ref,
    slope1_ref,
    slope2_ref,
    state_ref,
    z_ref,
    patch0_ref,
    patch1_ref,
    patch2_ref,
    patch3_ref,
    patch4_ref,
    masked0_ref,
    masked1_ref,
    upstream_ref,
    grad2_ref,
    total_ref,
):
    row = place_ref[0]
    col = place_ref[1]
    rates = [place_ref[2], place_ref[3], place_ref[4]]
    inside = lane_mask(col)
    patch_refs = (patch0_ref, patch1_ref, patch2_ref)
    slope_refs = (slope0_ref, slope1_ref, slope2_ref)
    parts = (part0_ref, part1_ref, part2_ref, part3_ref)
    w_out = w_out_ref[...]

    def activate(layer, base, state):
        block = pl.ds(base, ROWS)
        state_ref[block] = state
        act, slope = gelu_pair(state.astype(F32))
        slope_refs[layer][block] = slope.astype(BF16)
        act = act * rows_mask(inside, row, base, ROWS)
        patch_refs[layer][block] = shifted_rows(act, rates[layer])

    for n in range(4):

        def start(step, carry, n=n):
            at = ROWS * step
            given = parts[n][pl.ds(at, ROWS)].astype(F32)
            base = HALO * n + at
            activate(0, base, (mixed_ref[pl.ds(base, ROWS)] + given).astype(BF16))
            return carry

        lax.fori_loop(0, HALO // ROWS, start, 0)

    def next_state(base):
        block = pl.ds(base, ROWS)
        return (state_ref[block].astype(F32) + z_ref[block]).astype(BF16)

    for layer in (1, 2):

        def make(base, layer=layer):
            convolve(
                forward_ref[layer - 1], patch_refs[layer - 1], z_ref, base, ROWS, rates[layer - 1]
            )

        def use(base, layer=layer):
            activate(layer, base, next_state(base))

        pipelined(8 * layer, WIDE - 8 * layer, ROWS, make, use)

    for n in range(4):
        upstream_ref[HALO * n : HALO * n + HALO, :] = parts[n][32].astype(F32) + parts[n][33].astype(F32)
    tile_lanes = jnp.where(lax.broadcasted_iota(jnp.int32, (1, WIDE), 1) < TILE, 1.0, 0.0).astype(F32)

    def keep(ref, base, rounded):
        at = base + lax.broadcasted_iota(jnp.int32, (ROWS, 1, 1), 0)
        own = jnp.where((at >= HALO) & (at < HALO + TILE), 1.0, 0.0).astype(F32) * tile_lanes[None]
        ref[pl.ds(base, ROWS)] = (rounded.astype(F32) * own).astype(BF16)

    def first_grad(base):
        return upstream_ref[pl.ds(base, ROWS), :][:, None, :] * w_out[None]

    def last_make(base):
        convolve(forward_ref[2], patch2_ref, z_ref, base, ROWS, rates[2])

    def last_use(base):
        new = next_state(base).astype(F32)
        direct_ref[pl.ds(base - HALO, ROWS), :] = jnp.sum(new * w_out[None], axis=1)[:, :TILE]

    def begin(step):
        base = 8 + ROWS * step
        rounded = first_grad(base).astype(BF16)
        keep(masked0_ref, base, rounded)
        patch3_ref[pl.ds(base, ROWS)] = shifted_rows(rounded.astype(F32), rates[2])

    pipelined(HALO, HALO + TILE, ROWS, last_make, last_use, begin)
    for step in (3, 4, 5, 6):
        begin(step)

    total_ref[...] = jnp.zeros_like(total_ref)

    def weight_terms(layer, masked_ref, step):
        rate = rates[layer]
        total = total_ref[layer]
        for part in range(4):
            at = 24 + ROWS * step + 4 * part
            left = jnp.concatenate(
                [
                    jnp.concatenate([masked_ref[at + k + off] for k in range(4)], axis=1)
                    for off in (rate, 0, -rate)
                ],
                axis=0,
            )
            right = jnp.concatenate([patch_refs[layer][at + k] for k in range(4)], axis=1)
            total = total + lax.dot_general(
                left, right, (((1,), (1,)), ((), ())), preferred_element_type=F32
            )
        total_ref[layer] = total

    def second_make(base):
        convolve(backward_ref[2], patch3_ref, z_ref, base, ROWS, rates[2])

    def second_use(base):
        block = pl.ds(base, ROWS)
        new = first_grad(base) + z_ref[block] * slope2_ref[block].astype(F32)
        new = new * rows_mask(inside, row, base, ROWS)
        grad2_ref[block] = new
        rounded = new.astype(BF16)
        keep(masked1_ref, base, rounded)
        patch4_ref[block] = shifted_rows(rounded.astype(F32), rates[1])

    pipelined(16, 112, ROWS, second_make, second_use, lambda step: weight_terms(2, masked0_ref, step))

    first_half = lax.broadcasted_iota(jnp.int32, (1, 1, WIDE), 2) < TILE

    def third_make(base):
        convolve(backward_ref[1], patch4_ref, z_ref, base, ROWS, rates[1])

    def third_use(base):
        block = pl.ds(base, ROWS)
        new = grad2_ref[block] + z_ref[block] * slope1_ref[block].astype(F32)
        new = new * rows_mask(inside, row, base, ROWS)
        rounded = new.astype(BF16)
        keep(masked0_ref, base, rounded)
        last_ref[pl.ds(base - 24, ROWS)] = rounded
        slope = pltpu.roll(slope0_ref[block].astype(F32), TILE, 2)
        grad_ref[pl.ds(base - 24, ROWS)] = jnp.where(first_half, new, slope)

    done = pipelined(24, 104, ROWS, third_make, third_use, lambda step: weight_terms(1, masked1_ref, step))
    weight_terms(1, masked1_ref, done)
    for step in range(5):
        weight_terms(0, masked0_ref, step)
    terms = jnp.concatenate([total_ref[layer] for layer in range(3)], axis=0)
    spare = jnp.concatenate([terms[216:288, 32 * k : 32 * k + 32] for k in range(3)], axis=0)
    terms_ref[...] = jnp.concatenate([terms[0:216], spare], axis=1).astype(BF16)


def last_kernel(
    place_ref,
    grad_ref,
    round_ref,
    rows_ref,
    cols_ref,
    backward_ref,
    w_in_ref,
    row_ref,
    col_ref,
    z_ref,
    patch_ref,
    total_ref,
):
    rate = place_ref[2]

    def spread(step, carry):
        block = pl.ds(ROWS * step, ROWS)
        patch_ref[block] = shifted_rows(round_ref[block].astype(F32), rate)
        return carry

    lax.fori_loop(0, 80 // ROWS, spread, 0)
    w_in = w_in_ref[...]
    cols = cols_ref[0:TILE, :]

    def make(base):
        convolve(backward_ref[0], patch_ref, z_ref, base, ROWS, rate)

    def use(base):
        block = pl.ds(base, ROWS)
        both = grad_ref[block]
        slope = pltpu.roll(both, TILE, 2)
        start = (both + z_ref[block] * slope)[:, :, :TILE].astype(BF16)
        rows = rows_ref[pl.ds(base + 24, ROWS), :]
        sums = []
        total = total_ref[...]
        for k in range(ROWS):
            hidden = lax.dot_general(
                start[k], w_in, (((0,), (0,)), ((), ())), preferred_element_type=F32
            )
            outer = hidden * gelu_pair(rows[k : k + 1, :] + cols)[1]
            sums.append(jnp.sum(outer, axis=0, keepdims=True))
            total = total + outer
        total_ref[...] = total
        row_ref[pl.ds(base - 8, ROWS), :] = jnp.concatenate(sums, axis=0).astype(BF16)

    total_ref[...] = jnp.zeros_like(total_ref)
    pipelined(8, 8 + TILE, ROWS, make, use)
    col_ref[...] = total_ref[...].astype(BF16)


def finish_kernel(
    mine_ref,
    got_ref,
    col_ref,
    w_left_ref,
    w_right_ref,
    direct_ref,
    other_ref,
    logits_ref,
    grad_rows_ref,
    grad_cols_ref,
    conv_ref,
):
    logits_ref[...] = 0.5 * (direct_ref[...] + other_ref[...].T)
    total = mine_ref[...].astype(F32) + got_ref[...].astype(F32)
    for value, weight_ref, out_ref in (
        (total[0:TILE], w_left_ref, grad_rows_ref),
        (col_ref[...].astype(F32), w_right_ref, grad_cols_ref),
    ):
        out_ref[...] = lax.dot_general(
            value,
            weight_ref[...].astype(F32),
            (((1,), (1,)), ((), ())),
            precision=lax.Precision.HIGHEST,
            preferred_element_type=F32,
        )
    terms = total[TILE:] * (1.0 / 1024.0)
    spare = jnp.concatenate([terms[72 * k : 72 * k + 72, 96:128] for k in range(3)], axis=1)
    terms = jnp.concatenate([terms[:, 0:96], spare], axis=0)
    for layer in range(3):
        at = 96 * layer
        conv_ref[layer] = jnp.concatenate(
            [terms[at + CH * a : at + CH * a + CH] for a in range(3)], axis=1
        )


def shape(*dims, dtype=F32):
    return jax.ShapeDtypeStruct(dims, dtype)


def call(kernel, outs, specs, scratch=(), mib=8, cost=1):
    return pl.pallas_call(
        kernel,
        out_shape=outs,
        in_specs=specs,
        out_specs=[VMEM] * len(outs),
        scratch_shapes=list(scratch),
        compiler_params=pltpu.CompilerParams(vmem_limit_bytes=mib * 2**20),
        cost_estimate=pl.CostEstimate(
            flops=cost * 10**9, bytes_accessed=cost * 3 * 10**6, transcendentals=0
        ),
    )


def on_device(features, w_left, w_right, w_in, pair_input, conv_w, w_out, dilation, cotangent):
    n_row = lax.axis_size("row")
    n_col = lax.axis_size("col")
    row_at = lax.axis_index("row").astype(jnp.int32)
    col_at = lax.axis_index("col").astype(jnp.int32)
    place = jnp.concatenate([jnp.stack([row_at, col_at]), dilation, jnp.zeros((3,), jnp.int32)])
    up = [(i, i + 1) for i in range(n_row - 1)]
    down = [(i + 1, i) for i in range(n_row - 1)]
    swap = [(r * n_col + c, c * n_col + r) for r in range(n_row) for c in range(n_col)]

    mirrored = lax.ppermute(cotangent, ("row", "col"), swap)
    (sent,) = call(
        spread_kernel, [shape(n_row * n_col, *features.shape, dtype=BF16)], [VMEM]
    )(features)
    gathered = lax.all_to_all(sent, ("row", "col"), 0, 0)
    own, left_edge, right_edge, upstream = call(
        edges_kernel,
        [shape(TILE, CH, TILE, dtype=BF16)]
        + [shape(17, CH, WIDE, dtype=BF16)] * 2
        + [shape(TILE, TILE)],
        [VMEM] * 3,
        (),
        8,
        12,
    )(pair_input, cotangent, mirrored)
    from_left = lax.ppermute(right_edge, "col", up)
    from_right = lax.ppermute(left_edge, "col", down)

    upper, lower = call(
        widen_kernel, [shape(HALO + 2, CH, WIDE, dtype=BF16)] * 2, [VMEM] * 4
    )(own, upstream, from_left, from_right)
    above = lax.ppermute(lower, "row", up)
    below = lax.ppermute(upper, "row", down)

    mixed, row_project, col_project, backward_w = call(
        mixed_kernel,
        [shape(WIDE, CH, WIDE), shape(WIDE, 128), shape(WIDE, 128)]
        + [shape(3, CH, 288, dtype=BF16)],
        [SMEM] + [VMEM] * 5,
        [pltpu.VMEM((WIDE, 128), F32)],
        16,
        6,
    )(place, gathered, w_left, w_right, w_in, conv_w)
    w_out_wide = jnp.broadcast_to(w_out.astype(F32)[:, None], (CH, WIDE))
    big = (WIDE, CH, WIDE)
    direct, terms, grad, rounded = call(
        main_kernel,
        [shape(TILE, TILE), shape(216, 128, dtype=BF16), shape(80, CH, WIDE), shape(80, CH, WIDE, dtype=BF16)],
        [SMEM] + [VMEM] * 8,
        [pltpu.VMEM(big, BF16)] * 4
        + [pltpu.VMEM(big, F32)]
        + [pltpu.VMEM((WIDE, 96, WIDE), BF16)] * 5
        + [pltpu.VMEM(big, BF16)] * 2
        + [pltpu.VMEM((WIDE, WIDE), F32), pltpu.VMEM(big, F32), pltpu.VMEM((3, 96, 96), F32)],
        36,
        24,
    )(place, mixed, above, upper, lower, below, conv_w, backward_w, w_out_wide)

    def flipped(value, row_bits, col_bits):
        pairs = [
            (r * n_col + c, (r ^ row_bits) * n_col + (c ^ col_bits))
            for r in range(n_row)
            for c in range(n_col)
        ]
        return lax.ppermute(value, ("row", "col"), pairs)

    def summed(value, row_bits, col_bits):
        return (value.astype(F32) + flipped(value, row_bits, col_bits).astype(F32)).astype(BF16)

    direct_other = lax.ppermute(direct, ("row", "col"), swap)
    terms = summed(terms, 1, 0)
    grad, rounded, row_project, col_project, terms = lax.optimization_barrier(
        (grad, rounded, row_project, col_project, terms)
    )
    terms = summed(terms, 2, 0)
    row_part, col_part = call(
        last_kernel,
        [shape(TILE, 128, dtype=BF16), shape(TILE, 128, dtype=BF16)],
        [SMEM] + [VMEM] * 6,
        [
            pltpu.VMEM((80, CH, WIDE), F32),
            pltpu.VMEM((80, 96, WIDE), BF16),
            pltpu.VMEM((TILE, 128), F32),
        ],
        16,
        7,
    )(place, grad, rounded, row_project, col_project, backward_w, w_in)

    packed = jnp.concatenate([col_part, terms], axis=0)
    packed = summed(packed, 4, 0)
    row_part = summed(row_part, 0, 1)
    packed = summed(packed, 12, 0)
    col_part = packed[:TILE]
    terms = summed(packed[TILE:], 2, 1)
    col_part = summed(col_part, 1, 0)
    packed = jnp.concatenate([row_part, terms], axis=0)
    packed = summed(packed, 0, 2)
    col_part = summed(col_part, 2, 0)
    packed = summed(packed, 0, 4)
    return tuple(
        call(
            finish_kernel,
            [shape(TILE, TILE), shape(TILE, 128), shape(TILE, 128), shape(3, CH, 288)],
            [VMEM] * 7,
        )(packed, flipped(packed, 0, 12), col_part, w_left, w_right, direct, direct_other)
    )


def solution(mesh):
    return jax.shard_map(
        on_device,
        mesh=mesh,
        in_specs=(
            P(("row", "col"), None),
            P(),
            P(),
            P(),
            P(None, "row", "col"),
            P(),
            P(),
            P(),
            P("row", "col"),
        ),
        out_specs=(P("row", "col"), P("row", None), P("col", None), P()),
        check_vma=False,
    )
```

```python
import jax
import jax.numpy as jnp
from jax import lax
from jax.experimental import pallas as pl
from jax.experimental.pallas import tpu as pltpu
from jax.sharding import PartitionSpec as P

F32 = jnp.float32
BF16 = jnp.bfloat16
K_ROOT = 0.7978845608028654
CUBIC = 0.044715
TILE = 64
HALO = 32
WIDE = TILE + 2 * HALO
CH = 32
ROWS = 16
VMEM = pl.BlockSpec(memory_space=pltpu.VMEM)
SMEM = pl.BlockSpec(memory_space=pltpu.SMEM)


def gelu(value):
    inner = value * (K_ROOT + (K_ROOT * CUBIC) * (value * value))
    half = 0.5 * value
    return half + half * jnp.tanh(inner)


def gelu_pair(value):
    square = value * value
    tangent = jnp.tanh(value * (K_ROOT + (K_ROOT * CUBIC) * square))
    half = 0.5 * value
    up = 0.5 + 0.5 * tangent
    result = value * up
    slope = up + half * (1.0 - tangent * tangent) * (K_ROOT + (3.0 * K_ROOT * CUBIC) * square)
    return result, slope


def split(value):
    high = value.astype(BF16)
    return high, (value - high.astype(F32)).astype(BF16)


def spread_kernel(feat_ref, sent_ref):
    sent_ref[...] = jnp.broadcast_to(feat_ref[...][None], sent_ref.shape)


def edges_kernel(
    pair_ref, cot_ref, mirror_ref, own_ref, left_ref, right_ref, upstream_ref
):
    own = jnp.swapaxes(pair_ref[...].astype(F32), 0, 1)
    own_ref[...] = own.astype(BF16)
    cot = 0.5 * (cot_ref[...] + mirror_ref[...].T)
    upstream_ref[...] = cot
    for out_ref, first in ((left_ref, 0), (right_ref, TILE - HALO)):
        last = first + HALO
        for q in range(16):
            out_ref[q] = jnp.concatenate(
                [own[q + 16 * m, :, first:last] for m in range(4)], axis=1
            ).astype(BF16)
        edge = jnp.concatenate([cot[16 * m : 16 * m + 16, first:last] for m in range(4)], axis=1)
        high, low = split(edge)
        out_ref[16, 0:16, :] = high
        out_ref[16, 16:32, :] = low


def widen_kernel(own_ref, upstream_ref, from_left_ref, from_right_ref, upper_ref, lower_ref):
    cot = upstream_ref[...]
    for m in range(4):
        out_ref = (upper_ref, lower_ref)[m // 2]
        lanes = slice(HALO * m, HALO * m + HALO)
        base = 16 * (m % 2)
        for q in range(16):
            out_ref[base + q] = jnp.concatenate(
                [
                    own_ref[16 * m + q].astype(F32),
                    from_right_ref[q].astype(F32)[:, lanes],
                    from_left_ref[q].astype(F32)[:, lanes],
                ],
                axis=1,
            ).astype(BF16)
        high, low = split(cot[16 * m : 16 * m + 16, :])
        for part, row, at in ((high, 32, 0), (low, 33, 16)):
            out_ref[row, base : base + 16, :] = jnp.concatenate(
                [
                    part.astype(F32),
                    from_right_ref[16, at : at + 16, :].astype(F32)[:, lanes],
                    from_left_ref[16, at : at + 16, :].astype(F32)[:, lanes],
                ],
                axis=1,
            ).astype(BF16)


def mixed_kernel(
    place_ref, feat_ref, w_left_ref, w_right_ref, w_in_ref, conv_ref,
    mixed_ref, rows_ref, cols_ref, backward_ref, picked_ref,
):
    row = place_ref[0]
    col = place_ref[1]
    row_chunks = [jnp.maximum(2 * row - 1, 0), 2 * row, 2 * row + 1, jnp.minimum(2 * row + 2, 31)]
    col_chunks = [2 * col, 2 * col + 1, jnp.minimum(2 * col + 2, 31), jnp.maximum(2 * col - 1, 0)]
    for chunks, weight_ref, out_ref in (
        (row_chunks, w_left_ref, rows_ref),
        (col_chunks, w_right_ref, cols_ref),
    ):
        for n, chunk in enumerate(chunks):
            for m in range(8):
                at = HALO * n + 4 * m
                picked_ref[at : at + 4, :] = feat_ref[8 * chunk + m].astype(F32)
        out_ref[...] = jnp.dot(
            picked_ref[...].astype(BF16), weight_ref[...], preferred_element_type=F32
        )
    for layer in range(3):
        turned = jnp.concatenate([conv_ref[layer].astype(F32), jnp.zeros((CH, 96), F32)], axis=1)
        turned = jnp.concatenate([turned[:, 128 * k : 128 * k + 128].T for k in range(3)], axis=0)
        backward_ref[layer] = jnp.concatenate(
            [turned[CH * tap : CH * tap + CH] for tap in range(8, -1, -1)], axis=1
        ).astype(BF16)
    w_in = w_in_ref[...]

    def body(step, carry):
        cols = cols_ref[...]
        rows = rows_ref[pl.ds(ROWS * step, ROWS), :]
        for k in range(0, ROWS, 2):
            pair = [gelu(rows[k + i : k + i + 1, :] + cols).astype(BF16) for i in range(2)]
            out = lax.dot_general(
                w_in, jnp.concatenate(pair, 0), (((1,), (1,)), ((), ())), preferred_element_type=F32
            )
            for i in range(2):
                mixed_ref[ROWS * step + k + i] = out[:, WIDE * i : WIDE * i + WIDE]
        return carry

    lax.fori_loop(0, WIDE // ROWS, body, 0)


def lane_mask(col):
    lane = lax.broadcasted_iota(jnp.int32, (1, WIDE), 1)
    bin_at = TILE * col + jnp.where(lane < TILE + HALO, lane, lane - WIDE)
    return jnp.where((bin_at >= 0) & (bin_at < 1024), 1.0, 0.0).astype(F32)


def shifted_rows(value, rate):
    return jnp.concatenate(
        [pltpu.roll(value, rate, 2), value, pltpu.roll(value, WIDE - rate, 2)], axis=1
    ).astype(BF16)


def rows_mask(inside, row, base, rows):
    at = TILE * row - HALO + base + lax.broadcasted_iota(jnp.int32, (rows, 1, 1), 0)
    return jnp.where((at >= 0) & (at < 1024), 1.0, 0.0).astype(F32) * inside[None]


def convolve(weight, patch_ref, out_ref, base, rows, rate):
    for k in range(rows // 2):
        i = base + 2 * k
        taps = [
            jnp.concatenate([patch_ref[i + off], patch_ref[i + off + 1]], axis=1)
            for off in (-rate, 0, rate)
        ]
        z = jnp.dot(weight, jnp.concatenate(taps, axis=0), preferred_element_type=F32)
        out_ref[i] = z[:, :WIDE]
        out_ref[i + 1] = z[:, WIDE:]


def pipelined(first, last, rows, make, use, beside=None):
    make(first)

    def body(step, carry):
        base = first + rows * step
        use(base - rows)
        make(base)
        if beside is not None:
            beside(step - 1)
        return carry

    blocks = (last - first) // rows
    for step in range(1, blocks):
        body(step, 0)
    use(last - rows)
    return blocks - 1


def main_kernel(
    place_ref,
    mixed_ref,
    part0_ref,
    part1_ref,
    part2_ref,
    part3_ref,
    forward_ref,
    backward_ref,
    w_out_ref,
    direct_ref,
    terms_ref,
    grad_ref,
    last_ref,
    slope0_ref,
    slope1_ref,
    slope2_ref,
    state_ref,
    z_ref,
    patch0_ref,
    patch1_ref,
    patch2_ref,
    patch3_ref,
    patch4_ref,
    masked0_ref,
    masked1_ref,
    upstream_ref,
    grad2_ref,
    total_ref,
):
    row = place_ref[0]
    col = place_ref[1]
    rates = [place_ref[2], place_ref[3], place_ref[4]]
    inside = lane_mask(col)
    patch_refs = (patch0_ref, patch1_ref, patch2_ref)
    slope_refs = (slope0_ref, slope1_ref, slope2_ref)
    parts = (part0_ref, part1_ref, part2_ref, part3_ref)
    w_out = w_out_ref[...]

    def activate(layer, base, state):
        block = pl.ds(base, ROWS)
        state_ref[block] = state
        act, slope = gelu_pair(state.astype(F32))
        slope_refs[layer][block] = slope.astype(BF16)
        act = act * rows_mask(inside, row, base, ROWS)
        patch_refs[layer][block] = shifted_rows(act, rates[layer])

    for n in range(4):

        def start(step, carry, n=n):
            at = ROWS * step
            given = parts[n][pl.ds(at, ROWS)].astype(F32)
            base = HALO * n + at
            activate(0, base, (mixed_ref[pl.ds(base, ROWS)] + given).astype(BF16))
            return carry

        for step in range(HALO // ROWS):
            start(step, 0)

    def next_state(base):
        block = pl.ds(base, ROWS)
        return (state_ref[block].astype(F32) + z_ref[block]).astype(BF16)

    for layer in (1, 2):

        def make(base, layer=layer):
            convolve(
                forward_ref[layer - 1], patch_refs[layer - 1], z_ref, base, ROWS, rates[layer - 1]
            )

        def use(base, layer=layer):
            activate(layer, base, next_state(base))

        pipelined(8 * layer, WIDE - 8 * layer, ROWS, make, use)

    for n in range(4):
        upstream_ref[HALO * n : HALO * n + HALO, :] = parts[n][32].astype(F32) + parts[n][33].astype(F32)
    tile_lanes = jnp.where(lax.broadcasted_iota(jnp.int32, (1, WIDE), 1) < TILE, 1.0, 0.0).astype(F32)

    def keep(ref, base, rounded):
        at = base + lax.broadcasted_iota(jnp.int32, (ROWS, 1, 1), 0)
        own = jnp.where((at >= HALO) & (at < HALO + TILE), 1.0, 0.0).astype(F32) * tile_lanes[None]
        ref[pl.ds(base, ROWS)] = (rounded.astype(F32) * own).astype(BF16)

    def first_grad(base):
        return upstream_ref[pl.ds(base, ROWS), :][:, None, :] * w_out[None]

    def last_make(base):
        convolve(forward_ref[2], patch2_ref, z_ref, base, ROWS, rates[2])

    def last_use(base):
        new = next_state(base).astype(F32)
        direct_ref[pl.ds(base - HALO, ROWS), :] = jnp.sum(new * w_out[None], axis=1)[:, :TILE]

    def begin(step):
        base = 8 + ROWS * step
        rounded = first_grad(base).astype(BF16)
        keep(masked0_ref, base, rounded)
        patch3_ref[pl.ds(base, ROWS)] = shifted_rows(rounded.astype(F32), rates[2])

    pipelined(HALO, HALO + TILE, ROWS, last_make, last_use, begin)
    for step in (3, 4, 5, 6):
        begin(step)

    total_ref[...] = jnp.zeros_like(total_ref)

    def weight_terms(layer, masked_ref, step):
        rate = rates[layer]
        total = total_ref[layer]
        for part in range(4):
            at = 24 + ROWS * step + 4 * part
            left = jnp.concatenate(
                [
                    jnp.concatenate([masked_ref[at + k + off] for k in range(4)], axis=1)
                    for off in (rate, 0, -rate)
                ],
                axis=0,
            )
            right = jnp.concatenate([patch_refs[layer][at + k] for k in range(4)], axis=1)
            total = total + lax.dot_general(
                left, right, (((1,), (1,)), ((), ())), preferred_element_type=F32
            )
        total_ref[layer] = total

    def second_make(base):
        convolve(backward_ref[2], patch3_ref, z_ref, base, ROWS, rates[2])

    def second_use(base):
        block = pl.ds(base, ROWS)
        new = first_grad(base) + z_ref[block] * slope2_ref[block].astype(F32)
        new = new * rows_mask(inside, row, base, ROWS)
        grad2_ref[block] = new
        rounded = new.astype(BF16)
        keep(masked1_ref, base, rounded)
        patch4_ref[block] = shifted_rows(rounded.astype(F32), rates[1])

    pipelined(16, 112, ROWS, second_make, second_use, lambda step: weight_terms(2, masked0_ref, step))

    first_half = lax.broadcasted_iota(jnp.int32, (1, 1, WIDE), 2) < TILE

    def third_make(base):
        convolve(backward_ref[1], patch4_ref, z_ref, base, ROWS, rates[1])

    def third_use(base):
        block = pl.ds(base, ROWS)
        new = grad2_ref[block] + z_ref[block] * slope1_ref[block].astype(F32)
        new = new * rows_mask(inside, row, base, ROWS)
        rounded = new.astype(BF16)
        keep(masked0_ref, base, rounded)
        last_ref[pl.ds(base - 24, ROWS)] = rounded
        slope = pltpu.roll(slope0_ref[block].astype(F32), TILE, 2)
        grad_ref[pl.ds(base - 24, ROWS)] = jnp.where(first_half, new, slope)

    done = pipelined(24, 104, ROWS, third_make, third_use, lambda step: weight_terms(1, masked1_ref, step))
    weight_terms(1, masked1_ref, done)
    for step in range(5):
        weight_terms(0, masked0_ref, step)
    terms = jnp.concatenate([total_ref[layer] for layer in range(3)], axis=0)
    spare = jnp.concatenate([terms[216:288, 32 * k : 32 * k + 32] for k in range(3)], axis=0)
    terms_ref[0:208, :] = jnp.concatenate([terms[0:208], spare[0:208]], axis=1).astype(BF16)
    terms_ref[208:224, :] = jnp.concatenate(
        [jnp.concatenate([terms[208:216], spare[208:216]], axis=1), jnp.zeros((8, 128), F32)], axis=0
    ).astype(BF16)


def last_kernel(
    place_ref,
    grad_ref,
    round_ref,
    rows_ref,
    cols_ref,
    backward_ref,
    w_in_ref,
    row_ref,
    col_ref,
    z_ref,
    patch_ref,
    total_ref,
):
    rate = place_ref[2]

    def spread(step, carry):
        block = pl.ds(ROWS * step, ROWS)
        patch_ref[block] = shifted_rows(round_ref[block].astype(F32), rate)
        return carry

    lax.fori_loop(0, 80 // ROWS, spread, 0)
    w_in = w_in_ref[...]
    cols = cols_ref[0:TILE, :]

    def make(base):
        convolve(backward_ref[0], patch_ref, z_ref, base, ROWS, rate)

    def use(base):
        block = pl.ds(base, ROWS)
        both = grad_ref[block]
        slope = pltpu.roll(both, TILE, 2)
        start = (both + z_ref[block] * slope)[:, :, :TILE].astype(BF16)
        rows = rows_ref[pl.ds(base + 24, ROWS), :]
        sums = []
        total = total_ref[...]
        for k in range(ROWS):
            hidden = lax.dot_general(
                start[k], w_in, (((0,), (0,)), ((), ())), preferred_element_type=F32
            )
            outer = hidden * gelu_pair(rows[k : k + 1, :] + cols)[1]
            sums.append(jnp.sum(outer, axis=0, keepdims=True))
            total = total + outer
        total_ref[...] = total
        row_ref[pl.ds(base - 8, ROWS), :] = jnp.concatenate(sums, axis=0).astype(BF16)

    total_ref[...] = jnp.zeros_like(total_ref)
    pipelined(8, 8 + TILE, ROWS, make, use)
    col_ref[...] = total_ref[...].astype(BF16)


def finish_kernel(
    place_ref,
    mine_ref,
    got_ref,
    col_ref,
    w_left_ref,
    w_right_ref,
    direct_ref,
    other_ref,
    logits_ref,
    grad_rows_ref,
    grad_cols_ref,
    conv_ref,
):
    logits_ref[...] = 0.5 * (direct_ref[...] + other_ref[...].T)
    total = mine_ref[...].astype(F32)
    mine = total[TILE:]
    other = got_ref[...].astype(F32)
    second = place_ref[0] % 2 == 1
    for value, weight_ref, out_ref in (
        (total[0:TILE], w_left_ref, grad_rows_ref),
        (col_ref[...].astype(F32), w_right_ref, grad_cols_ref),
    ):
        out_ref[...] = lax.dot_general(
            value,
            weight_ref[...].astype(F32),
            (((1,), (1,)), ((), ())),
            precision=lax.Precision.HIGHEST,
            preferred_element_type=F32,
        )
    terms = jnp.concatenate(
        [jnp.where(second, other, mine), jnp.where(second, mine, other)], axis=0
    )[0:216] * (1.0 / 1024.0)
    spare = jnp.concatenate([terms[72 * k : 72 * k + 72, 96:128] for k in range(3)], axis=1)
    terms = jnp.concatenate([terms[:, 0:96], spare], axis=0)
    for layer in range(3):
        at = 96 * layer
        conv_ref[layer] = jnp.concatenate(
            [terms[at + CH * a : at + CH * a + CH] for a in range(3)], axis=1
        )


def shape(*dims, dtype=F32):
    return jax.ShapeDtypeStruct(dims, dtype)


def call(kernel, outs, specs, scratch=(), mib=8, cost=1):
    return pl.pallas_call(
        kernel,
        out_shape=outs,
        in_specs=specs,
        out_specs=[VMEM] * len(outs),
        scratch_shapes=list(scratch),
        compiler_params=pltpu.CompilerParams(vmem_limit_bytes=mib * 2**20),
        cost_estimate=pl.CostEstimate(
            flops=cost * 10**9, bytes_accessed=cost * 3 * 10**6, transcendentals=0
        ),
    )


def on_device(features, w_left, w_right, w_in, pair_input, conv_w, w_out, dilation, cotangent):
    n_row = lax.axis_size("row")
    n_col = lax.axis_size("col")
    row_at = lax.axis_index("row").astype(jnp.int32)
    col_at = lax.axis_index("col").astype(jnp.int32)
    place = jnp.concatenate([jnp.stack([row_at, col_at]), dilation, jnp.zeros((3,), jnp.int32)])
    up = [(i, i + 1) for i in range(n_row - 1)]
    down = [(i + 1, i) for i in range(n_row - 1)]
    swap = [(r * n_col + c, c * n_col + r) for r in range(n_row) for c in range(n_col)]

    mirrored = lax.ppermute(cotangent, ("row", "col"), swap)
    (sent,) = call(
        spread_kernel, [shape(n_row * n_col, *features.shape, dtype=BF16)], [VMEM]
    )(features)
    gathered = lax.all_to_all(sent, ("row", "col"), 0, 0)
    own, left_edge, right_edge, upstream = call(
        edges_kernel,
        [shape(TILE, CH, TILE, dtype=BF16)]
        + [shape(17, CH, WIDE, dtype=BF16)] * 2
        + [shape(TILE, TILE)],
        [VMEM] * 3,
        (),
        8,
        12,
    )(pair_input, cotangent, mirrored)
    from_left = lax.ppermute(right_edge, "col", up)
    from_right = lax.ppermute(left_edge, "col", down)

    upper, lower = call(
        widen_kernel, [shape(HALO + 2, CH, WIDE, dtype=BF16)] * 2, [VMEM] * 4
    )(own, upstream, from_left, from_right)
    above = lax.ppermute(lower, "row", up)
    below = lax.ppermute(upper, "row", down)

    mixed, row_project, col_project, backward_w = call(
        mixed_kernel,
        [shape(WIDE, CH, WIDE), shape(WIDE, 128), shape(WIDE, 128)]
        + [shape(3, CH, 288, dtype=BF16)],
        [SMEM] + [VMEM] * 5,
        [pltpu.VMEM((WIDE, 128), F32)],
        16,
        6,
    )(place, gathered, w_left, w_right, w_in, conv_w)
    w_out_wide = jnp.broadcast_to(w_out.astype(F32)[:, None], (CH, WIDE))
    big = (WIDE, CH, WIDE)
    direct, terms, grad, rounded = call(
        main_kernel,
        [shape(TILE, TILE), shape(224, 128, dtype=BF16), shape(80, CH, WIDE), shape(80, CH, WIDE, dtype=BF16)],
        [SMEM] + [VMEM] * 8,
        [pltpu.VMEM(big, BF16)] * 4
        + [pltpu.VMEM(big, F32)]
        + [pltpu.VMEM((WIDE, 96, WIDE), BF16)] * 5
        + [pltpu.VMEM(big, BF16)] * 2
        + [pltpu.VMEM((WIDE, WIDE), F32), pltpu.VMEM(big, F32), pltpu.VMEM((3, 96, 96), F32)],
        36,
        24,
    )(place, mixed, above, upper, lower, below, conv_w, backward_w, w_out_wide)

    def flipped(value, row_bits, col_bits):
        pairs = [
            (r * n_col + c, (r ^ row_bits) * n_col + (c ^ col_bits))
            for r in range(n_row)
            for c in range(n_col)
        ]
        return lax.ppermute(value, ("row", "col"), pairs)

    def summed(value, row_bits, col_bits):
        return (value.astype(F32) + flipped(value, row_bits, col_bits).astype(F32)).astype(BF16)

    direct_other = lax.ppermute(direct, ("row", "col"), swap)
    second = row_at % 2 == 1
    terms = jnp.where(second, terms[112:], terms[:112]).astype(F32) + flipped(
        jnp.where(second, terms[:112], terms[112:]), 1, 0
    ).astype(F32)
    terms = terms.astype(BF16)
    grad, rounded, row_project, col_project, terms = lax.optimization_barrier(
        (grad, rounded, row_project, col_project, terms)
    )
    terms = summed(terms, 2, 0)
    row_part, col_part = call(
        last_kernel,
        [shape(TILE, 128, dtype=BF16), shape(TILE, 128, dtype=BF16)],
        [SMEM] + [VMEM] * 6,
        [
            pltpu.VMEM((80, CH, WIDE), F32),
            pltpu.VMEM((80, 96, WIDE), BF16),
            pltpu.VMEM((TILE, 128), F32),
        ],
        16,
        7,
    )(place, grad, rounded, row_project, col_project, backward_w, w_in)

    packed = jnp.concatenate([col_part, terms], axis=0)
    packed = summed(packed, 4, 0)
    row_part = summed(row_part, 0, 1)
    packed = summed(packed, 12, 0)
    col_part = packed[:TILE]
    terms = summed(packed[TILE:], 2, 1)
    col_part = summed(col_part, 1, 0)
    packed = jnp.concatenate([row_part, terms], axis=0)
    packed = summed(packed, 0, 2)
    col_part = summed(col_part, 2, 0)
    packed = summed(packed, 0, 4)
    packed = summed(packed, 0, 12)
    return tuple(
        call(
            finish_kernel,
            [shape(TILE, TILE), shape(TILE, 128), shape(TILE, 128), shape(3, CH, 288)],
            [SMEM] + [VMEM] * 7,
        )(place, packed, flipped(packed[TILE:], 1, 0), col_part, w_left, w_right, direct, direct_other)
    )


def solution(mesh):
    return jax.shard_map(
        on_device,
        mesh=mesh,
        in_specs=(
            P(("row", "col"), None),
            P(),
            P(),
            P(),
            P(None, "row", "col"),
            P(),
            P(),
            P(),
            P("row", "col"),
        ),
        out_specs=(P("row", "col"), P("row", None), P("col", None), P()),
        check_vma=False,
    )
```
